256 devices in a mesh: row: 32 (over y, x, core), col: 8 (over z).
Axes of the slice: x: 4, y: 4, z: 8, core: 2. Of those that a mesh axis runs over, the one named last changes fastest.
Arguments:
- x_state: float32 [64, 262144], P(None, ('row', 'col')), may hold values from -6 to 6
- p_state: float32 [64, 262144], P(None, ('row', 'col')), may hold values from -6 to 6
- ax_state: float32 [64, 262144], P(None, ('row', 'col')), may hold values from -27 to 27
- ap_state: float32 [64, 262144], P(None, ('row', 'col')), may hold values from -27 to 27
- stiff_diag: float32 [64, 262144], P(None, ('row', 'col')), may hold values from 1 to 72
- tiles: float32 [64, 9437184], P(None, ('row', 'col')), may hold values from -0.1875 to 0.1875
- tile_rows: int32 [147456], P(('row', 'col')), may hold values from 0 to 47, as said below
- tile_cols: int32 [147456], P(('row', 'col')), may hold values from 0 to 127
- tile_count: int32 [256], P(('row', 'col')), may hold values from 144 to 576, as said below
- rotation: float32 [2, 192, 64], replicated, may hold values from -1.5 to 1.5
Outputs:
- next_x: float32 [64, 262144], P(None, ('row', 'col'))
- next_p: float32 [64, 262144], P(None, ('row', 'col'))
- next_ax: float32 [64, 262144], P(None, ('row', 'col'))
- next_ap: float32 [64, 262144], P(None, ('row', 'col'))
- grams: float32 [2, 2, 192, 192], replicated
The draws below stay inside these ranges and needn't reach their ends.
Inputs may be any that keep to these rules, and one draw needn't show every extreme that they name: `tile_rows`: the devices with row index 0 have no slot with local row under 16, those with the last row index none at 32 or over. `tile_count`: values of slots at or past a device's count are to be ignored; some device is full.
All inputs are finite; a program needn't handle non-finite values.
Results may differ from the reference program's by a relative error of at most 0.0003.
Values sent between devices are 32-bit elements; how exact they have to be, the bound alone decides.
A program may use at most 192 MiB of HBM per device.

```python
import math
import jax
import jax.numpy as jnp
from jax import lax

MODES = 64
TILE = 64
BPD = 16
ITERS = 2
MAXT = 576
DOFS = 262144
N_ROW = 32
N_COL = 8
DEVICES = 256


def tile_pattern(key):
    slots = DEVICES * MAXT
    key_piece, key_block, key_col, key_count, key_busy = jax.random.split(key, 5)
    device = jnp.arange(slots, dtype=jnp.int32) // MAXT
    row_group_index = device // N_COL
    pick = jax.random.randint(key_piece, (slots,), 0, 6)
    piece = jnp.where(pick == 0, 0, jnp.where(pick == 5, 2, 1))
    piece = jnp.where((row_group_index == 0) & (piece == 0), 1, piece)
    piece = jnp.where((row_group_index == N_ROW - 1) & (piece == 2), 1, piece)
    rows = piece * BPD + jax.random.randint(key_block, (slots,), 0, BPD)
    cols = jax.random.randint(key_col, (slots,), 0, N_COL * BPD)
    counts = jax.random.randint(key_count, (DEVICES,), MAXT // 4, MAXT + 1)
    busy = jax.random.randint(key_busy, (), 0, DEVICES)
    counts = jnp.where(jnp.arange(DEVICES, dtype=jnp.int32) == busy, MAXT, counts)
    return (rows.astype(jnp.int32), cols.astype(jnp.int32), counts.astype(jnp.int32))


def state_pair(key):
    key_mode, key_factor, key_noise = jax.random.split(key, 3)
    shape = (MODES, DOFS)
    modes = jnp.clip(jax.random.normal(key_mode, shape, jnp.float32), -4.0, 4.0)
    factor = jnp.exp(jax.random.uniform(key_factor, shape, jnp.float32) * math.log(4.0))
    noise = 0.5 * jnp.clip(jax.random.normal(key_noise, shape, jnp.float32), -4.0, 4.0)
    return (modes, modes * factor + noise)


def draw_tile_rows(key, part):
    return tile_pattern(key)[0]


def draw_tile_cols(key, part):
    return tile_pattern(key)[1]


def draw_tile_count(key, part):
    return tile_pattern(key)[2]


def draw_x_state(key, part):
    return state_pair(jax.random.fold_in(key, 10))[0]


def draw_ax_state(key, part):
    return state_pair(jax.random.fold_in(key, 10))[1]


def draw_p_state(key, part):
    return state_pair(jax.random.fold_in(key, 20))[0]


def draw_ap_state(key, part):
    return state_pair(jax.random.fold_in(key, 20))[1]


def draw_stiff_diag(key, part):
    key = jax.random.fold_in(key, 3)
    spread = jax.random.uniform(key, (MODES, DOFS), jnp.float32)
    position = jnp.arange(DOFS, dtype=jnp.float32)[None, :] / DOFS
    return jnp.exp(spread * math.log(8.0)) * (1.0 + 2.0 * position)


def draw_rotation(key, part):
    key = jax.random.fold_in(key, 5)
    shape = (ITERS, 3 * MODES, MODES)
    ident = (jnp.arange(3 * MODES)[:, None] == jnp.arange(MODES)[None, :]).astype(jnp.float32)
    noise = jnp.clip(jax.random.normal(key, shape, jnp.float32), -4.0, 4.0)
    return 0.8 * ident[None] + 0.4 / math.sqrt(MODES) * noise


def block_levels(own_key, dims, shards, low, largest):
    loudness = 1.0
    for axis_at, blocks in shards:
        draws = jax.random.uniform(jax.random.fold_in(jax.random.fold_in(own_key, 6), axis_at), (blocks,), jnp.float32, low / len(shards), largest / len(shards))
        loudness = loudness * jnp.repeat(jnp.exp(draws), dims[axis_at] // blocks).reshape((-1,) + (1,) * (len(dims) - 1 - axis_at))
    return loudness


def gaussian(own_key, extent, deviation, reach, cuts=(), kind=jnp.bfloat16):
    factor_of = block_levels(own_key, extent, cuts, -0.22, 0.18) if cuts else 1.0
    result = jax.random.normal(own_key, extent, jnp.float32) * deviation * factor_of
    return jnp.minimum(jnp.maximum(result, -reach), reach).astype(kind)


def setup_inputs(seed: int = 0) -> dict:
    seeds = jax.random.split(jax.random.key(seed), 11)
    x_state = draw_x_state(jax.random.fold_in(seeds[10], 71), 0)
    p_state = draw_p_state(jax.random.fold_in(seeds[10], 71), 0)
    ax_state = draw_ax_state(jax.random.fold_in(seeds[10], 71), 0)
    ap_state = draw_ap_state(jax.random.fold_in(seeds[10], 71), 0)
    stiff_diag = draw_stiff_diag(jax.random.fold_in(seeds[10], 71), 0)
    tiles = gaussian(seeds[5], (TILE, DEVICES * MAXT * TILE), (TILE * MAXT // (2 * BPD)) ** -0.5, 0.1875, ((1, 256),), jnp.float32)
    tile_rows = draw_tile_rows(jax.random.fold_in(seeds[10], 71), 0)
    tile_cols = draw_tile_cols(jax.random.fold_in(seeds[10], 71), 0)
    tile_count = draw_tile_count(jax.random.fold_in(seeds[10], 71), 0)
    rotation = draw_rotation(jax.random.fold_in(seeds[10], 71), 0)
    return {"x_state": x_state, "p_state": p_state, "ax_state": ax_state, "ap_state": ap_state, "stiff_diag": stiff_diag, "tiles": tiles, "tile_rows": tile_rows, "tile_cols": tile_cols, "tile_count": tile_count, "rotation": rotation}


PRECISION_TOP = lax.Precision.HIGHEST


def stiffness(field, tiles, tile_rows, tile_cols, tile_count, stiff_diag):
    blocks_all = DOFS // TILE
    blocked = field.reshape(MODES, blocks_all, TILE).transpose(1, 0, 2)

    def one_device(total, device):
        group_row = device // N_COL
        group_column_index = device % N_COL
        start = device * MAXT
        rows = lax.dynamic_slice_in_dim(tile_rows, start, MAXT)
        cols = lax.dynamic_slice_in_dim(tile_cols, start, MAXT)
        values = lax.dynamic_slice_in_dim(tiles, start * TILE, MAXT * TILE, 1).reshape(TILE, MAXT, TILE)
        piece = rows // BPD
        inner = rows % BPD
        global_row = ((group_row - 1 + piece) * N_COL + group_column_index) * BPD + inner
        global_col = group_row * N_COL * BPD + cols
        live = (jnp.arange(MAXT, dtype=jnp.int32) < tile_count[device]).astype(jnp.float32)
        matrix_product = jnp.einsum("tme,ate->tma", blocked[global_col], values, precision=PRECISION_TOP)
        matrix_product = matrix_product * live[:, None, None]
        return total.at[global_row].add(matrix_product), None

    start_total = jnp.zeros((blocks_all, MODES, TILE), jnp.float32)
    total, unused = lax.scan(one_device, start_total, jnp.arange(DEVICES, dtype=jnp.int32))
    return total.transpose(1, 0, 2).reshape(MODES, DOFS) + stiff_diag * field


def reference(x_state, p_state, ax_state, ap_state, stiff_diag, tiles, tile_rows, tile_cols, tile_count, rotation):
    modes_now, search_now = x_state, p_state
    image_now, search_image = ax_state, ap_state
    grams_all = []
    for step in range(ITERS):
        rayleigh_block = jnp.einsum("mn,kn->mk", modes_now, image_now, precision=PRECISION_TOP) / DOFS
        residual = image_now - jnp.einsum("mk,mn->kn", rayleigh_block, modes_now, precision=PRECISION_TOP)
        correction = residual / stiff_diag
        correction_image = stiffness(correction, tiles, tile_rows, tile_cols, tile_count, stiff_diag)
        basis = jnp.concatenate([modes_now, correction, search_now], axis=0)
        basis_stiff_image = jnp.concatenate([image_now, correction_image, search_image], axis=0)
        gram_a = jnp.einsum("kn,ln->kl", basis, basis_stiff_image, precision=PRECISION_TOP) / DOFS
        gram_b = jnp.einsum("kn,ln->kl", basis, basis, precision=PRECISION_TOP) / DOFS
        grams_all.append(jnp.stack([gram_a, gram_b]))
        rotation_now = rotation[step]
        modes_now = jnp.einsum("kj,kn->jn", rotation_now, basis, precision=PRECISION_TOP)
        image_now = jnp.einsum("kj,kn->jn", rotation_now, basis_stiff_image, precision=PRECISION_TOP)
        search_now = jnp.einsum("kj,kn->jn", rotation_now[MODES:], basis[MODES:], precision=PRECISION_TOP)
        search_image = jnp.einsum("kj,kn->jn", rotation_now[MODES:], basis_stiff_image[MODES:], precision=PRECISION_TOP)
    return modes_now, search_now, image_now, search_image, jnp.stack(grams_all)
```

```python
import functools

import jax
import jax.numpy as jnp
from jax import lax
from jax.experimental import pallas as pl
from jax.experimental.pallas import tpu as pltpu
from jax.sharding import PartitionSpec as P

F32 = jnp.float32
BF16 = jnp.bfloat16
MESH = pl.DeviceIdType.MESH
DMA = pltpu.SemaphoreType.DMA

MODES, TILE, BPD, SLOTS = 64, 64, 16, 576
NROW, NCOL = 32, 8
LOCAL = TILE * BPD
DOFS = LOCAL * NROW * NCOL
PLANE, DEEP = 8, 4
SIZES = {"xc": PLANE, "y": DEEP, "z": NCOL}
LANES = 128
STRIPS = LOCAL // LANES
BLOCKS = NCOL * BPD
WIDE = BLOCKS * TILE
PARTS = 4
HOPS = 3 * PARTS + PARTS // 2
CHUNKS, PAIRS = 4, 12


def halves(value):
    high = value.astype(BF16)
    return high, (value - high.astype(F32)).astype(BF16)


def product(a, b, dims):
    dot = functools.partial(
        lax.dot_general, dimension_numbers=(dims, ((), ())), preferred_element_type=F32
    )
    a_high, a_low = halves(a)
    b_high, b_low = halves(b)
    return dot(a_high, b_high) + (dot(a_high, b_low) + dot(a_low, b_high))


NN = ((1,), (0,))
NT = ((1,), (1,))
TN = ((0,), (0,))


class Place:
    def __init__(self):
        i, j = lax.axis_index("row"), lax.axis_index("col")
        self.i, self.j = i, j
        plane, inner = i // PLANE, lax.rem(i, PLANE)
        self.groups = {
            "xc": (PLANE, inner, lambda m: (plane * PLANE + m, j)),
            "y": (DEEP, plane, lambda m: (m * PLANE + inner, j)),
            "z": (NCOL, j, lambda m: (i, m)),
        }
        self.next_row = (lax.rem(i + 1, NROW), j)
        self.last_row = (lax.rem(i + NROW - 1, NROW), j)
        self.right = (i, lax.rem(j + 1, NCOL))
        self.left = (i, lax.rem(j + NCOL - 1, NCOL))


def greet(place, rows):
    barrier = pltpu.get_barrier_semaphore()
    devices = [place.next_row, place.last_row] if rows else []
    for size, me, device in place.groups.values():
        devices += [device(lax.rem(me + o, size)) for o in range(1, size)]
    for device in devices:
        pl.semaphore_signal(barrier, inc=1, device_id=device, device_id_type=MESH)
    return lambda: pl.semaphore_wait(barrier, len(devices))


def swap(place, name, source, landing, sends, recvs):
    size, me, device = place.groups[name]
    copies = []
    for o in range(1, size):
        peer = lax.rem(me + o, size)
        copy = pltpu.make_async_remote_copy(
            src_ref=source(peer),
            dst_ref=landing.at[me],
            send_sem=sends.at[o],
            recv_sem=recvs.at[o],
            device_id=device(peer),
            device_id_type=MESH,
        )
        copy.start()
        copies.append(copy)
    return copies


def finish(copies):
    for copy in copies:
        copy.wait()


def total(landing):
    value = landing[0]
    for m in range(1, landing.shape[0]):
        value = value + landing[m]
    return value


def theta_scratch():
    shapes = [pltpu.VMEM((SIZES[n], 32, LANES), F32) for n in SIZES]
    return shapes + [DMA((SIZES[n],)) for n in SIZES for _ in range(2)]


def sum_theta(place, local, scratch):
    value = jnp.concatenate([local[:32], local[32:]], axis=1)
    for at, name in enumerate(SIZES):
        landing, sends, recvs = scratch[at], scratch[3 + 2 * at], scratch[4 + 2 * at]
        me = place.groups[name][1]
        landing[me] = value
        finish(swap(place, name, lambda peer: landing.at[me], landing, sends, recvs))
        value = total(landing)
    return jnp.concatenate([value[:, :64], value[:, 64:]], axis=0)


STAGES = ("xc", "y", "z", "y", "xc")


def mix_scratch(rows):
    r = rows // NROW
    big, mid = (PLANE, DEEP, r, LANES), (DEEP, r, LANES)
    shapes = [big, big, mid, mid, (NCOL, r, LANES), mid, big]
    return [pltpu.VMEM(s, F32) for s in shapes] + [
        DMA((SIZES[n],)) for n in STAGES for _ in range(2)
    ]


def mix(place, rows, flat, scratch):
    r = rows // NROW
    data, land_a, half, land_b, land_z, back, result = scratch[:7]
    sems = [scratch[7 + 2 * n : 9 + 2 * n] for n in range(5)]
    mine = {name: place.groups[name][1] for name in SIZES}
    for a in range(PLANE):
        for b in range(DEEP):
            at = (a * DEEP + b) * r
            data[a, b] = flat[at : at + r, :]
    land_a[mine["xc"]] = data[mine["xc"]]
    copies = swap(place, "xc", lambda peer: data.at[peer], land_a, *sems[0])
    yield
    finish(copies)
    half[...] = total(land_a)
    land_b[mine["y"]] = half[mine["y"]]
    copies = swap(place, "y", lambda peer: half.at[peer], land_b, *sems[1])
    yield
    finish(copies)
    land_z[mine["z"]] = total(land_b)
    copies = swap(place, "z", lambda peer: land_z.at[mine["z"]], land_z, *sems[2])
    yield
    finish(copies)
    back[mine["y"]] = total(land_z)
    copies = swap(place, "y", lambda peer: back.at[mine["y"]], back, *sems[3])
    yield
    finish(copies)
    result[mine["xc"]] = back[...]
    copies = swap(place, "xc", lambda peer: result.at[mine["xc"]], result, *sems[4])
    yield
    finish(copies)


def unmix(rows, result, flat):
    r = rows // NROW
    for a in range(PLANE):
        for b in range(DEEP):
            at = (a * DEEP + b) * r
            flat[at : at + r, :] = result[a, b]


def ring_scratch():
    return [
        pltpu.VMEM((NCOL, STRIPS, MODES, LANES), F32),
        DMA((2, HOPS)),
        DMA((2, HOPS)),
    ]


def ring(place, scratch, spread_ref, beside=None):
    held, sends, recvs = scratch
    per = STRIPS // PARTS
    devices = (place.right, place.left)

    def region(way, n, hop):
        q, s = n // PARTS, lax.rem(n, PARTS)
        if way == 0:
            return lax.rem(place.j + 2 * NCOL - q - hop, NCOL), s
        return lax.rem(place.j + q + hop, NCOL), PARTS - 1 - s

    def copy(way, n, hop=0):
        slot, part = region(way, n, hop)
        piece = held.at[slot, pl.ds(part * per, per)]
        return pltpu.make_async_remote_copy(
            src_ref=piece,
            dst_ref=piece,
            send_sem=sends.at[way, n],
            recv_sem=recvs.at[way, n],
            device_id=devices[way],
            device_id_type=MESH,
        )

    def spread(slot, first, count):
        def one(b, carry):
            value = held[slot, first + b]
            high = value.astype(BF16).astype(F32)
            at = pl.multiple_of((slot * STRIPS + first + b) * LANES, LANES)
            both = jnp.concatenate([high, value - high], axis=0)
            spread_ref[pl.ds(at, LANES), :] = both.T.astype(BF16)
            return carry

        lax.fori_loop(0, count, one, 0)

    def begin(n, carry):
        for way in range(2):
            copy(way, n).start()
        return carry

    def step(n, carry):
        for way in range(2):
            copy(way, n, 1).wait_recv()

            @pl.when(n + PARTS < HOPS)
            def forward():
                copy(way, n + PARTS).start()

        for way in range(2):
            slot, part = region(way, n, 1)
            spread(slot, part * per, per)
        return carry

    def end(n, carry):
        for way in range(2):
            copy(way, n).wait_send()
        return carry

    lax.fori_loop(0, PARTS, begin, 0)
    if beside is not None:
        next(beside)
    spread_ref[WIDE : WIDE + TILE, :] = jnp.zeros((TILE, LANES), BF16)
    spread(place.j, 0, STRIPS)
    stops = (0, 4, 6, 8, 10, HOPS) if beside is not None else (0, HOPS)
    for a, b in zip(stops[:-1], stops[1:]):
        lax.fori_loop(a, b, step, 0)
        if beside is not None:
            next(beside, None)
    if beside is not None:
        for _ in beside:
            pass
    lax.fori_loop(0, HOPS, end, 0)


def correct(place, x_ref, ax_ref, diag_ref, theta_t, w_ref, held):
    for s in range(STRIPS):
        at = slice(s * LANES, (s + 1) * LANES)
        residual = ax_ref[:, at] - product(theta_t, x_ref[:, at], NN)
        w = residual / diag_ref[:, at]
        w_ref[:, at] = w
        held[place.j, s] = w


def theta_local(x_ref, ax_ref):
    return product(ax_ref[...], x_ref[...], NT) * (1.0 / DOFS)


def fold(value):
    return jnp.concatenate([value[:96], value[96:]], axis=1)


def gram_rest(x_ref, w_ref, p_ref, ax_ref, ap_ref, flat, base):
    basis = jnp.concatenate([x_ref[...], w_ref[...], p_ref[...]], axis=0)
    other = jnp.concatenate([ax_ref[...], ap_ref[...], basis], axis=0)
    block = product(basis, other, NT) * (1.0 / DOFS)
    flat[base : base + 192, :] = block[:, :128]
    flat[base + 192 : base + 384, :] = block[:, 128:256]
    flat[base + 384 : base + 480, :] = fold(block[:, 256:])


def gram_image(x_ref, w_ref, p_ref, aw_ref, flat):
    basis = jnp.concatenate([x_ref[...], w_ref[...], p_ref[...]], axis=0)
    flat[0:96, :] = fold(product(basis, aw_ref[...], NT) * (1.0 / DOFS))


def halo_scratch():
    return [pltpu.VMEM((MODES, LOCAL), F32)] * 2 + [DMA((2,)), DMA((2,))]


def halo(place, part_ref, scratch):
    above, below, sends, recvs = scratch
    copies = []
    for at, (first, landing, device) in enumerate(
        ((0, above, place.last_row), (2 * LOCAL, below, place.next_row))
    ):
        copy = pltpu.make_async_remote_copy(
            src_ref=part_ref.at[:, pl.ds(first, LOCAL)],
            dst_ref=landing,
            send_sem=sends.at[at],
            recv_sem=recvs.at[at],
            device_id=device,
            device_id_type=MESH,
        )
        copy.start()
        copies.append(copy)
    return copies


def image(part_ref, w_ref, diag_ref, above, below, aw_ref):
    aw_ref[...] = (
        part_ref[:, LOCAL : 2 * LOCAL]
        + below[...]
        + above[...]
        + diag_ref[...] * w_ref[...]
    )


def rotate(turn, x, w, p, next_x, next_p):
    moved = product(turn[64:], jnp.concatenate([w[...], p[...]], axis=0), TN)
    next_p[...] = moved
    next_x[...] = product(turn[:64], x[...], TN) + moved


def opening(x, p, ax, ap, diag, w, spread_ref, sums, *scratch):
    place = Place()
    ready = greet(place, rows=False)
    theta = scratch[:9]
    ring_set = scratch[9:12]
    flat = scratch[12]
    mixing = scratch[13:]
    local = theta_local(x, ax)
    ready()
    theta_t = sum_theta(place, local, theta)
    correct(place, x, ax, diag, theta_t, w, ring_set[0])

    def beside():
        gram_rest(x, w, p, ax, ap, flat, 0)
        yield from mix(place, 480, flat, mixing)
        sums[...] = mixing[6][...]

    ring(place, ring_set, spread_ref, beside())


def middle(
    part, turn, x, w, p, ax, ap, diag,
    x1, w1, p1, ax1, ap1, spread_ref, sums, *scratch,
):
    place = Place()
    ready = greet(place, rows=True)
    theta = scratch[:9]
    ring_set = scratch[9:12]
    flat, aw = scratch[12:14]
    around = scratch[14:18]
    mixing = scratch[18:]
    ready()
    copies = halo(place, part, around)
    rotate(turn[0], x, w, p, x1, p1)
    finish(copies)
    image(part, w, diag, around[0], around[1], aw)
    rotate(turn[0], ax, aw, ap, ax1, ap1)
    theta_t = sum_theta(place, theta_local(x1, ax1), theta)
    correct(place, x1, ax1, diag, theta_t, w1, ring_set[0])

    def beside():
        gram_image(x, w, p, aw, flat)
        gram_rest(x1, w1, p1, ax1, ap1, flat, 96)
        yield from mix(place, 576, flat, mixing)
        sums[...] = mixing[6][...]

    ring(place, ring_set, spread_ref, beside())


def put_grams(rest, image_block, grams, k):
    left = jnp.concatenate([image_block[:, :64], image_block[:, 64:]], axis=0)
    block = rest[0:192]
    grams[k, 0] = jnp.concatenate([block[:, :64], left, block[:, 64:]], axis=1)
    tail = rest[384:480]
    grams[k, 1] = jnp.concatenate(
        [rest[192:384], jnp.concatenate([tail[:, :64], tail[:, 64:]], axis=0)], axis=1
    )


def closing(
    part, turn, x, w, p, ax, ap, diag, sums0, sums1,
    x2, p2, ax2, ap2, grams, *scratch,
):
    place = Place()
    ready = greet(place, rows=True)
    flat, aw, flat0, flat1 = scratch[:4]
    around = scratch[4:8]
    mixing = scratch[8:]
    ready()
    copies = halo(place, part, around)
    unmix(480, sums0, flat0)
    unmix(576, sums1, flat1)
    put_grams(flat0[...], flat1[0:96], grams, 0)
    rotate(turn[1], x, w, p, x2, p2)
    finish(copies)
    image(part, w, diag, around[0], around[1], aw)
    gram_image(x, w, p, aw, flat)
    steps = mix(place, 96, flat, mixing)
    next(steps)
    rotate(turn[1], ax, aw, ap, ax2, ap2)
    for _ in steps:
        pass
    unmix(96, mixing[6], flat)
    put_grams(flat1[96:576], flat[0:96], grams, 1)


def sparse(cols, rows, count, tiles, spread_ref, part, total_ref):
    step = pl.program_id(0)
    pairs = SLOTS // 2 // CHUNKS

    @pl.when(step == 0)
    def clear():
        total_ref[...] = jnp.zeros_like(total_ref)

    live = count[0]
    left = jnp.clip((live - step * pairs * 2 + 1) // 2, 0, pairs)
    nothing = jnp.zeros((TILE, LANES), BF16)

    def block(slot):
        column = jnp.where(slot < live, cols[slot], BLOCKS)
        return spread_ref[pl.ds(pl.multiple_of(column * TILE, TILE), TILE), :]

    def some(s, carry):
        found = []
        for u in range(PAIRS):
            q = s * PAIRS + u
            slot = (step * pairs + q) * 2
            high, low = halves(tiles[:, pl.ds(pl.multiple_of(q * LANES, LANES), LANES)])
            table = jnp.concatenate(
                [
                    jnp.concatenate([block(slot), nothing], axis=1),
                    jnp.concatenate([nothing, block(slot + 1)], axis=1),
                ],
                axis=0,
            )
            out = jnp.dot(
                jnp.concatenate([high, low], axis=0), table, preferred_element_type=F32
            )
            out = out[:TILE] + out[TILE:]
            found.append((rows[slot], out[:, :LANES]))
            found.append((rows[slot + 1], out[:, LANES:]))
        for row, value in found:
            total_ref[row] += value
        return carry

    lax.fori_loop(0, (left + PAIRS - 1) // PAIRS, some, 0)

    @pl.when(step == CHUNKS - 1)
    def write():
        def one(b, carry):
            both = jnp.concatenate([total_ref[2 * b], total_ref[2 * b + 1]], axis=0).T
            at = pl.multiple_of(b * LANES, LANES)
            part[:, pl.ds(at, LANES)] = both[:MODES] + both[MODES:]
            return carry

        lax.fori_loop(0, 3 * BPD // 2, one, 0, unroll=4)


FIELD = jax.ShapeDtypeStruct((MODES, LOCAL), F32)
SPREAD = jax.ShapeDtypeStruct((WIDE + TILE, LANES), BF16)


def talking(kernel, outs, scratch, number):
    whole = pl.BlockSpec(memory_space=pltpu.VMEM)
    return lambda *args: pl.pallas_call(
        kernel,
        out_shape=outs,
        in_specs=[whole] * len(args),
        out_specs=[whole] * len(outs),
        scratch_shapes=scratch,
        compiler_params=pltpu.CompilerParams(
            collective_id=number, has_side_effects=True, vmem_limit_bytes=48 << 20
        ),
        name=kernel.__name__,
    )(*args)


def sparse_product(cols, rows, count, tiles, spread_value):
    return pl.pallas_call(
        sparse,
        grid_spec=pltpu.PrefetchScalarGridSpec(
            num_scalar_prefetch=3,
            grid=(CHUNKS,),
            in_specs=[
                pl.BlockSpec((TILE, SLOTS * TILE // CHUNKS), lambda g, *_: (0, g)),
                pl.BlockSpec((WIDE + TILE, LANES), lambda g, *_: (0, 0)),
            ],
            out_specs=pl.BlockSpec((MODES, 3 * LOCAL), lambda g, *_: (0, 0)),
            scratch_shapes=[pltpu.VMEM((3 * BPD, TILE, LANES), F32)],
        ),
        out_shape=jax.ShapeDtypeStruct((MODES, 3 * LOCAL), F32),
        compiler_params=pltpu.CompilerParams(vmem_limit_bytes=48 << 20),
        name="sparse",
    )(cols, rows, count, tiles, spread_value)


def sums_of(rows):
    return jax.ShapeDtypeStruct((PLANE, DEEP, rows // NROW, LANES), F32)


def flat_of(rows):
    return pltpu.VMEM((rows, LANES), F32)


def body(x, p, ax, ap, diag, tiles, rows, cols, count, turns):
    field = pltpu.VMEM((MODES, LOCAL), F32)
    w, spread0, sums0 = talking(
        opening,
        [FIELD, SPREAD, sums_of(480)],
        theta_scratch() + ring_scratch() + [flat_of(480)] + mix_scratch(480),
        1,
    )(x, p, ax, ap, diag)
    part = sparse_product(cols, rows, count, tiles, spread0)
    x1, w1, p1, ax1, ap1, spread1, sums1 = talking(
        middle,
        [FIELD] * 5 + [SPREAD, sums_of(576)],
        theta_scratch()
        + ring_scratch()
        + [flat_of(576), field]
        + halo_scratch()
        + mix_scratch(576),
        2,
    )(part, turns, x, w, p, ax, ap, diag)
    part1 = sparse_product(cols, rows, count, tiles, spread1)
    return talking(
        closing,
        [FIELD] * 4 + [jax.ShapeDtypeStruct((2, 2, 192, 192), F32)],
        [flat_of(96), field, flat_of(480), flat_of(576)]
        + halo_scratch()
        + mix_scratch(96),
        3,
    )(part1, turns, x1, w1, p1, ax1, ap1, diag, sums0, sums1)


def solution(mesh):
    split = P(None, ("row", "col"))
    listed = P(("row", "col"))
    return jax.shard_map(
        lambda *args: tuple(body(*args)),
        mesh=mesh,
        in_specs=(split,) * 6 + (listed,) * 3 + (P(),),
        out_specs=(split,) * 4 + (P(),),
        check_vma=False,
    )
```

```python
import functools

import jax
import jax.numpy as jnp
from jax import lax
from jax.experimental import pallas as pl
from jax.experimental.pallas import tpu as pltpu
from jax.sharding import PartitionSpec as P

F32 = jnp.float32
I32 = jnp.int32
BF16 = jnp.bfloat16
MESH = pl.DeviceIdType.MESH
DMA = pltpu.SemaphoreType.DMA

MODES, TILE, BPD, SLOTS = 64, 64, 16, 576
NROW, NCOL = 32, 8
LOCAL = TILE * BPD
DOFS = LOCAL * NROW * NCOL
PLANE, DEEP = 8, 4
SIZES = {"xc": PLANE, "y": DEEP, "z": NCOL}
LANES = 128
STRIPS = LOCAL // LANES
BLOCKS = NCOL * BPD
ROWS = 3 * BPD
PARTS = 4
HOPS = 3 * PARTS + PARTS // 2
RANKS = 640
PAIRS = SLOTS // 2 + ROWS // 2
BATCH = 24
FRESH = 1 << 18


def halves(value):
    high = value.astype(BF16)
    return high, (value - high.astype(F32)).astype(BF16)


def product(a, b, dims):
    dot = functools.partial(
        lax.dot_general, dimension_numbers=(dims, ((), ())), preferred_element_type=F32
    )
    a_high, a_low = halves(a)
    b_high, b_low = halves(b)
    return dot(a_high, b_high) + (dot(a_high, b_low) + dot(a_low, b_high))


NN = ((1,), (0,))
NT = ((1,), (1,))
TN = ((0,), (0,))


class Place:
    def __init__(self):
        i, j = lax.axis_index("row"), lax.axis_index("col")
        self.i, self.j = i, j
        plane, inner = i // PLANE, lax.rem(i, PLANE)
        self.groups = {
            "xc": (PLANE, inner, lambda m: (plane * PLANE + m, j)),
            "y": (DEEP, plane, lambda m: (m * PLANE + inner, j)),
            "z": (NCOL, j, lambda m: (i, m)),
        }
        self.next_row = (lax.rem(i + 1, NROW), j)
        self.last_row = (lax.rem(i + NROW - 1, NROW), j)
        self.right = (i, lax.rem(j + 1, NCOL))
        self.left = (i, lax.rem(j + NCOL - 1, NCOL))


def greet(place, rows):
    barrier = pltpu.get_barrier_semaphore()
    devices = [place.next_row, place.last_row] if rows else []
    for size, me, device in place.groups.values():
        devices += [device(lax.rem(me + o, size)) for o in range(1, size)]
    for device in devices:
        pl.semaphore_signal(barrier, inc=1, device_id=device, device_id_type=MESH)
    return lambda: pl.semaphore_wait(barrier, len(devices))


def swap(place, name, source, landing, sends, recvs):
    size, me, device = place.groups[name]
    copies = []
    for o in range(1, size):
        peer = lax.rem(me + o, size)
        copy = pltpu.make_async_remote_copy(
            src_ref=source(peer),
            dst_ref=landing.at[me],
            send_sem=sends.at[o],
            recv_sem=recvs.at[o],
            device_id=device(peer),
            device_id_type=MESH,
        )
        copy.start()
        copies.append(copy)
    return copies


def finish(copies):
    for copy in copies:
        copy.wait()


def total(landing):
    value = landing[0]
    for m in range(1, landing.shape[0]):
        value = value + landing[m]
    return value


class Scratch:
    def __init__(self, shapes):
        self.names, self.shapes = list(shapes), list(shapes.values())

    def found(self, refs):
        return dict(zip(self.names, refs))


def sum_theta(place, local, refs, tag, work):
    value = jnp.concatenate([local[:32], local[32:]], axis=1)
    for at, name in enumerate(SIZES):
        landing = refs[f"{tag}_{name}"]
        me = place.groups[name][1]
        landing[me] = value
        copies = swap(
            place,
            name,
            lambda peer: landing.at[me],
            landing,
            refs[f"{tag}_{name}_s"],
            refs[f"{tag}_{name}_r"],
        )
        work[at]()
        finish(copies)
        value = total(landing)
    return jnp.concatenate([value[:, :64], value[:, 64:]], axis=0)


def theta_scratch(tag):
    shapes = {}
    for name, size in SIZES.items():
        shapes[f"{tag}_{name}"] = pltpu.VMEM((size, 32, LANES), F32)
        shapes[f"{tag}_{name}_s"] = DMA((size,))
        shapes[f"{tag}_{name}_r"] = DMA((size,))
    return shapes


STAGES = ("xc", "y", "z", "y", "xc")


def mix_scratch(tag, rows):
    r = rows // NROW
    big, mid = (PLANE, DEEP, r, LANES), (DEEP, r, LANES)
    shapes = {
        f"{tag}_{n}": pltpu.VMEM(s, F32)
        for n, s in enumerate((big, big, mid, mid, (NCOL, r, LANES), mid, big))
    }
    for n, name in enumerate(STAGES):
        shapes[f"{tag}_s{n}"] = DMA((SIZES[name],))
        shapes[f"{tag}_r{n}"] = DMA((SIZES[name],))
    return shapes


def mix(place, rows, flat, refs, tag):
    r = rows // NROW
    data, land_a, half, land_b, land_z, back, result = (refs[f"{tag}_{n}"] for n in range(7))
    sems = [(refs[f"{tag}_s{n}"], refs[f"{tag}_r{n}"]) for n in range(5)]
    mine = {name: place.groups[name][1] for name in SIZES}
    for a in range(PLANE):
        for b in range(DEEP):
            at = (a * DEEP + b) * r
            data[a, b] = flat[at : at + r, :]
    land_a[mine["xc"]] = data[mine["xc"]]
    copies = swap(place, "xc", lambda peer: data.at[peer], land_a, *sems[0])
    yield
    finish(copies)
    half[...] = total(land_a)
    land_b[mine["y"]] = half[mine["y"]]
    copies = swap(place, "y", lambda peer: half.at[peer], land_b, *sems[1])
    yield
    finish(copies)
    land_z[mine["z"]] = total(land_b)
    copies = swap(place, "z", lambda peer: land_z.at[mine["z"]], land_z, *sems[2])
    yield
    finish(copies)
    back[mine["y"]] = total(land_z)
    copies = swap(place, "y", lambda peer: back.at[mine["y"]], back, *sems[3])
    yield
    finish(copies)
    result[mine["xc"]] = back[...]
    copies = swap(place, "xc", lambda peer: result.at[mine["xc"]], result, *sems[4])
    yield
    finish(copies)
    for a in range(PLANE):
        for b in range(DEEP):
            at = (a * DEEP + b) * r
            flat[at : at + r, :] = result[a, b]
    yield


def short_scratch(tag, rows):
    r = rows // PLANE
    shapes = {
        f"{tag}_{n}": pltpu.VMEM((size, r, LANES), F32)
        for n, size in enumerate((PLANE, PLANE, DEEP, NCOL, PLANE))
    }
    for n, name in enumerate(("xc", "y", "z", "xc")):
        shapes[f"{tag}_s{n}"] = DMA((SIZES[name],))
        shapes[f"{tag}_r{n}"] = DMA((SIZES[name],))
    return shapes


def mix_short(place, rows, flat, refs, tag):
    r = rows // PLANE
    data, land_a, land_b, land_z, result = (refs[f"{tag}_{n}"] for n in range(5))
    sems = [(refs[f"{tag}_s{n}"], refs[f"{tag}_r{n}"]) for n in range(4)]
    mine = {name: place.groups[name][1] for name in SIZES}
    for a in range(PLANE):
        data[a] = flat[a * r : (a + 1) * r, :]
    land_a[mine["xc"]] = data[mine["xc"]]
    copies = swap(place, "xc", lambda peer: data.at[peer], land_a, *sems[0])
    yield
    finish(copies)
    land_b[mine["y"]] = total(land_a)
    copies = swap(place, "y", lambda peer: land_b.at[mine["y"]], land_b, *sems[1])
    yield
    finish(copies)
    land_z[mine["z"]] = total(land_b)
    copies = swap(place, "z", lambda peer: land_z.at[mine["z"]], land_z, *sems[2])
    yield
    finish(copies)
    result[mine["xc"]] = total(land_z)
    copies = swap(place, "xc", lambda peer: result.at[mine["xc"]], result, *sems[3])
    yield
    finish(copies)
    for a in range(PLANE):
        flat[a * r : (a + 1) * r, :] = result[a]
    yield


def ring_scratch(tag):
    return {
        f"{tag}_held": pltpu.VMEM((NCOL, STRIPS, MODES, LANES), F32),
        f"{tag}_s": DMA((2, HOPS)),
        f"{tag}_r": DMA((2, HOPS)),
    }


def ring(place, refs, tag, spread_ref, first, each):
    held, sends, recvs = refs[f"{tag}_held"], refs[f"{tag}_s"], refs[f"{tag}_r"]
    per = STRIPS // PARTS
    devices = (place.right, place.left)

    def region(way, n, hop):
        q, s = n // PARTS, lax.rem(n, PARTS)
        if way == 0:
            return lax.rem(place.j + 2 * NCOL - q - hop, NCOL), s
        return lax.rem(place.j + q + hop, NCOL), PARTS - 1 - s

    def copy(way, n, hop=0):
        slot, part = region(way, n, hop)
        piece = held.at[slot, pl.ds(part * per, per)]
        return pltpu.make_async_remote_copy(
            src_ref=piece,
            dst_ref=piece,
            send_sem=sends.at[way, n],
            recv_sem=recvs.at[way, n],
            device_id=devices[way],
            device_id_type=MESH,
        )

    def spread(slot, first, count):
        def one(b, carry):
            value = held[slot, first + b]
            high = value.astype(BF16).astype(F32)
            at = 2 * (slot * STRIPS + first + b) + 1
            both = jnp.concatenate([high, value - high], axis=0).T.astype(BF16)
            spread_ref[at] = both[:TILE]
            spread_ref[at + 1] = both[TILE:]
            return carry

        lax.fori_loop(0, count, one, 0)

    def begin(n, carry):
        for way in range(2):
            copy(way, n).start()
        return carry

    def step(n, carry):
        for way in range(2):
            copy(way, n, 1).wait_recv()

            @pl.when(n + PARTS < HOPS)
            def forward():
                copy(way, n + PARTS).start()

        for way in range(2):
            slot, part = region(way, n, 1)
            spread(slot, part * per, per)
        each(n)
        return carry

    def end(n, carry):
        for way in range(2):
            copy(way, n).wait_send()
        return carry

    lax.fori_loop(0, PARTS, begin, 0)
    first()
    spread(place.j, 0, STRIPS)
    lax.fori_loop(0, HOPS, step, 0)
    lax.fori_loop(0, HOPS, end, 0)


def line(ref):
    value = ref[...].reshape(1, SLOTS)
    return jnp.concatenate([value, jnp.zeros((1, RANKS - SLOTS), I32)], axis=1)


def upright(value):
    return jnp.broadcast_to(value, (LANES, RANKS)).T


def count_of(where, value=1):
    return jnp.sum(jnp.where(where, value, 0), axis=0, keepdims=True)


def order(rows, cols, live):
    lane = lax.broadcasted_iota(I32, (1, RANKS), 1)
    row = jnp.where(lane < live, rows, 255)
    below = lax.broadcasted_iota(I32, (RANKS, LANES), 0)
    row_up = upright(row)
    rank = []
    for b in range(RANKS // LANES):
        here = lax.broadcasted_iota(I32, (RANKS, LANES), 1) + b * LANES
        same = (row_up == row[:, b * LANES : (b + 1) * LANES]) & (below < here)
        rank.append(count_of(same))
    rank = jnp.concatenate(rank, axis=1)
    name = lax.broadcasted_iota(I32, (RANKS, LANES), 1)
    held = count_of(row_up == name)
    pairs = jnp.right_shift(held + 1, 1)
    pairs_up = jnp.broadcast_to(pairs, (LANES, LANES)).T[:ROWS]
    named = lax.broadcasted_iota(I32, (ROWS, RANKS), 0)
    wide_pairs = jnp.concatenate([pairs_up] * (RANKS // LANES), axis=1)
    start = count_of(named < row, wide_pairs)
    place = jnp.where(lane < live, 2 * start + rank, 5000)
    code = lane + 1024 * (cols + 1) + jnp.where(rank == 0, FRESH, 0)
    place_up, code_up = upright(place), upright(code)
    found = []
    for b in range(RANKS // LANES):
        here = lax.broadcasted_iota(I32, (RANKS, LANES), 1) + b * LANES
        found.append(count_of(place_up == here, code_up))
    mine = lax.broadcasted_iota(I32, (ROWS, LANES), 0)
    at = lax.broadcasted_iota(I32, (ROWS, LANES), 1)
    ends = jnp.where(pairs > 0, count_of(mine <= at, pairs_up), 0)
    return jnp.concatenate(found, axis=1), ends


def pack_pair(p, codes, tiles, packed):
    half = jnp.right_shift(lax.broadcasted_iota(I32, (TILE, LANES), 1), 6)

    def one(place, wanted):
        slot = jnp.bitwise_and(codes[0, place], 1023)
        value = tiles[:, pl.ds(jnp.right_shift(slot, 1) * LANES, LANES)]
        odd = jnp.broadcast_to(jnp.bitwise_and(slot, 1), (TILE, LANES))
        return jnp.where(odd == wanted, value, pltpu.roll(value, TILE, 1))

    both = jnp.where(half == 0, one(2 * p, 0), one(2 * p + 1, 1))
    packed[p] = jnp.concatenate(halves(both), axis=1)


def multiply(codes, ends, packed, spread_ref, sums, part, after):
    def batch(s, run):
        found = []
        for u in range(BATCH):
            p = s * BATCH + u
            pair = (codes[0, 2 * p], codes[0, 2 * p + 1])
            tables = []
            for code in pair:
                tables.append(spread_ref[jnp.bitwise_and(jnp.right_shift(code, 10), 255)])
            out = jnp.dot(
                packed[p], jnp.concatenate(tables * 2, axis=0), preferred_element_type=F32
            )
            fresh = jnp.broadcast_to(pair[0], (TILE, LANES)) >= FRESH
            found.append((p, fresh, out))
        for p, fresh, out in found:
            run = jnp.where(fresh, 0.0, run) + out
            sums[p + 1] = run
        return run

    sums[0] = jnp.zeros((TILE, LANES), F32)
    lax.fori_loop(0, PAIRS // BATCH, batch, jnp.zeros((TILE, LANES), F32))

    def place(b, carry):
        both = jnp.concatenate([sums[ends[0, 2 * b]], sums[ends[0, 2 * b + 1]]], axis=0).T
        part[:, pl.ds(pl.multiple_of(b * LANES, LANES), LANES)] = both[:MODES] + both[MODES:]
        return carry

    for third in (0, 2, 1):
        lax.fori_loop(third * STRIPS, (third + 1) * STRIPS, place, 0)
        after(third)


def correct(place, x, ax, diag, theta_t, w, held):
    for s in range(STRIPS):
        at = slice(s * LANES, (s + 1) * LANES)
        value = (ax[:, at] - product(theta_t, x[:, at], NN)) / diag[:, at]
        w[:, at] = value
        held[place.j, s] = value


def theta_local(x, ax):
    return product(ax[...], x[...], NT) * (1.0 / DOFS)


def fold(value):
    return jnp.concatenate([value[:96], value[96:]], axis=1)


def unfold(value):
    return jnp.concatenate([value[:, :64], value[:, 64:]], axis=0)


def gram_rest(x, w, p, ax, ap, flat, base):
    basis = jnp.concatenate([x[...], w[...], p[...]], axis=0)
    other = jnp.concatenate([ax[...], ap[...], basis], axis=0)
    block = product(basis, other, NT) * (1.0 / DOFS)
    flat[base : base + 192, :] = block[:, :128]
    flat[base + 192 : base + 384, :] = block[:, 128:256]
    flat[base + 384 : base + 480, :] = fold(block[:, 256:])


def gram_image(x, w, p, aw, flat):
    basis = jnp.concatenate([x[...], w[...], p[...]], axis=0)
    flat[0:96, :] = fold(product(basis, aw[...], NT) * (1.0 / DOFS))


def halo_scratch(tag):
    return {
        f"{tag}_above": pltpu.VMEM((MODES, LOCAL), F32),
        f"{tag}_below": pltpu.VMEM((MODES, LOCAL), F32),
        f"{tag}_s": DMA((2,)),
        f"{tag}_r": DMA((2,)),
    }


def halo(place, part, refs, tag, third):
    at = third // 2
    copy = pltpu.make_async_remote_copy(
        src_ref=part.at[:, pl.ds(third * LOCAL, LOCAL)],
        dst_ref=refs[f"{tag}_below" if at else f"{tag}_above"],
        send_sem=refs[f"{tag}_s"].at[at],
        recv_sem=refs[f"{tag}_r"].at[at],
        device_id=place.next_row if at else place.last_row,
        device_id_type=MESH,
    )
    copy.start()
    return copy


def image(part, w, diag, refs, tag, aw):
    aw[...] = (
        part[:, LOCAL : 2 * LOCAL]
        + refs[f"{tag}_below"][...]
        + refs[f"{tag}_above"][...]
        + diag[...] * w[...]
    )


def rotate(turn, x, w, p, next_x, next_p):
    moved = product(turn[:, 64:], jnp.concatenate([w[...], p[...]], axis=0), NN)
    next_p[...] = moved
    next_x[...] = product(turn[:, :64], x[...], NN) + moved


def put_grams(rest, image_block, grams, k):
    block = rest[0:192]
    grams[k, 0] = jnp.concatenate([block[:, :64], unfold(image_block), block[:, 64:]], axis=1)
    grams[k, 1] = jnp.concatenate([rest[192:384], unfold(rest[384:480])], axis=1)


FIELDS = ("x", "ax", "diag", "p", "ap")
FIELD = pltpu.VMEM((MODES, LOCAL), F32)
NAMED = Scratch(
    {name: FIELD for name in FIELDS}
    | {f"{n}{k}": FIELD for k in (1, 2) for n in ("x", "p", "ax", "ap")}
    | {name: FIELD for name in ("w", "w1", "aw", "aw1")}
    | {
        "turn": pltpu.VMEM((2, MODES, 3 * MODES), F32),
        "tiles": pltpu.VMEM((TILE, SLOTS * TILE), F32),
        "loads": DMA((7,)),
        "stores": DMA((6,)),
        "codes_v": pltpu.VMEM((1, RANKS), I32),
        "ends_v": pltpu.VMEM((1, LANES), I32),
        "codes": pltpu.SMEM((1, RANKS), I32),
        "ends": pltpu.SMEM((1, LANES), I32),
        "lists": DMA((2,)),
        "packed": pltpu.VMEM((PAIRS, TILE, 2 * LANES), BF16),
        "sums": pltpu.VMEM((PAIRS + 1, TILE, LANES), F32),
        "spread": pltpu.VMEM((BLOCKS + 1, TILE, LANES), BF16),
        "part": pltpu.VMEM((MODES, 3 * LOCAL), F32),
        "flat0": pltpu.VMEM((480, LANES), F32),
        "flat1": pltpu.VMEM((576, LANES), F32),
        "flat2": pltpu.VMEM((96, LANES), F32),
        "grams": pltpu.VMEM((2, 2, 192, 192), F32),
    }
    | theta_scratch("theta0")
    | theta_scratch("theta1")
    | ring_scratch("ring0")
    | ring_scratch("ring1")
    | halo_scratch("halo0")
    | halo_scratch("halo1")
    | mix_scratch("mix0", 480)
    | mix_scratch("mix1", 576)
    | short_scratch("mix2", 96)
)
BESIDE_Y, BESIDE_Z = 72, 200


def steps(
    rows, cols, count, x_in, ax_in, diag_in, p_in, ap_in, turn_in, tiles_in,
    x_out, p_out, ax_out, ap_out, grams_out, *refs,
):
    place = Place()
    ready = greet(place, rows=True)
    r = NAMED.found(refs)
    loads = {}
    for n, (name, source) in enumerate(
        zip(FIELDS + ("turn", "tiles"), (x_in, ax_in, diag_in, p_in, ap_in, turn_in, tiles_in))
    ):
        loads[name] = pltpu.make_async_copy(source, r[name], r["loads"].at[n])
        loads[name].start()
    stores = []

    def store(source, target):
        copy = pltpu.make_async_copy(source, target, r["stores"].at[len(stores)])
        copy.start()
        stores.append(copy)

    codes, ends, packed, tiles = r["codes"], r["ends"], r["packed"], r["tiles"]
    x, ax, diag, p, ap = (r[name] for name in FIELDS)
    w, w1, aw, aw1, part, spread_ref = (
        r[n] for n in ("w", "w1", "aw", "aw1", "part", "spread")
    )

    def nothing(*unused):
        pass

    def sort():
        code, end = order(line(rows), line(cols), count[0])
        r["codes_v"][...] = code
        r["ends_v"][...] = end
        moves = [
            pltpu.make_async_copy(r["codes_v"], codes, r["lists"].at[0]),
            pltpu.make_async_copy(r["ends_v"], ends, r["lists"].at[1]),
        ]
        for move in moves:
            move.start()
        for move in moves:
            move.wait()
        spread_ref[0] = jnp.zeros((TILE, LANES), BF16)

    def pack(a, b):
        def four(s, carry):
            for u in range(4):
                pack_pair(4 * s + u, codes, tiles, packed)
            return carry

        return lambda: lax.fori_loop(a // 4, b // 4, four, 0)

    def pack_first():
        loads["tiles"].wait()
        pack(0, BESIDE_Y)()

    loads["x"].wait()
    loads["ax"].wait()
    local = theta_local(x, ax)
    ready()
    theta_t = sum_theta(
        place, local, r, "theta0", (sort, pack_first, pack(BESIDE_Y, BESIDE_Z))
    )
    loads["diag"].wait()
    correct(place, x, ax, diag, theta_t, w, r["ring0_held"])
    loads["p"].wait()
    loads["ap"].wait()
    loads["turn"].wait()
    mix0 = mix(place, 480, r["flat0"], r, "mix0")
    mix1 = mix(place, 576, r["flat1"], r, "mix1")
    mix2 = mix_short(place, 96, r["flat2"], r, "mix2")

    def first0():
        gram_rest(x, w, p, ax, ap, r["flat0"], 0)
        next(mix0)

    def each0(n):
        for u in range(8):
            pack_pair(BESIDE_Z + n * 8 + u, codes, tiles, packed)

    ring(place, r, "ring0", spread_ref, first0, each0)
    next(mix0)
    sent = []

    def send(tag):
        return lambda third: third == 1 or sent.append(halo(place, part, r, tag, third))

    multiply(codes, ends, packed, spread_ref, r["sums"], part, send("halo0"))
    next(mix0)
    x1, p1, ax1, ap1 = (r[n] for n in ("x1", "p1", "ax1", "ap1"))
    rotate(r["turn"][0], x, w, p, x1, p1)
    finish(sent)
    image(part, w, diag, r, "halo0", aw)
    rotate(r["turn"][0], ax, aw, ap, ax1, ap1)
    theta_t = sum_theta(
        place,
        theta_local(x1, ax1),
        r,
        "theta1",
        (nothing, lambda: gram_image(x, w, p, aw, r["flat1"]), lambda: next(mix0)),
    )
    correct(place, x1, ax1, diag, theta_t, w1, r["ring1_held"])

    def first1():
        gram_rest(x1, w1, p1, ax1, ap1, r["flat1"], 96)
        next(mix1)

    ring(place, r, "ring1", spread_ref, first1, nothing)
    next(mix1)
    next(mix0)
    sent = []
    multiply(codes, ends, packed, spread_ref, r["sums"], part, send("halo1"))
    next(mix1)
    x2, p2, ax2, ap2 = (r[n] for n in ("x2", "p2", "ax2", "ap2"))
    rotate(r["turn"][1], x1, w1, p1, x2, p2)
    store(x2, x_out)
    store(p2, p_out)
    finish(sent)
    image(part, w1, diag, r, "halo1", aw1)
    gram_image(x1, w1, p1, aw1, r["flat2"])
    next(mix2)
    next(mix1)
    rotate(r["turn"][1], ax1, aw1, ap1, ax2, ap2)
    store(ax2, ax_out)
    store(ap2, ap_out)
    next(mix2)
    next(mix1)
    next(mix0)
    next(mix2)
    next(mix1)
    put_grams(r["flat0"][...], r["flat1"][0:96], r["grams"], 0)
    store(r["grams"].at[0], grams_out.at[0])
    next(mix2)
    next(mix2)
    put_grams(r["flat1"][96:576], r["flat2"][...], r["grams"], 1)
    store(r["grams"].at[1], grams_out.at[1])
    for copy in stores:
        copy.wait()


def body(x, p, ax, ap, diag, tiles, rows, cols, count, turns):
    field = jax.ShapeDtypeStruct((MODES, LOCAL), F32)
    far = pl.BlockSpec(memory_space=pl.ANY)
    found = pl.pallas_call(
        steps,
        out_shape=[field] * 4 + [jax.ShapeDtypeStruct((2, 2, 192, 192), F32)],
        in_specs=[
            pl.BlockSpec(memory_space=pltpu.VMEM),
            pl.BlockSpec(memory_space=pltpu.VMEM),
            pl.BlockSpec(memory_space=pltpu.SMEM),
        ]
        + [far] * 7,
        out_specs=[far] * 5,
        scratch_shapes=NAMED.shapes,
        compiler_params=pltpu.CompilerParams(
            collective_id=1, has_side_effects=True, vmem_limit_bytes=60 << 20
        ),
        name="steps",
    )(rows, cols, count, x, ax, diag, p, ap, turns.swapaxes(1, 2), tiles)
    return pl.pallas_call(
        hand_over,
        out_shape=[jax.ShapeDtypeStruct(f.shape, f.dtype) for f in found],
        in_specs=[far] * 5,
        out_specs=[far] * 5,
        scratch_shapes=[pltpu.VMEM(f.shape, f.dtype) for f in found] + [DMA((5,))] * 2,
        compiler_params=pltpu.CompilerParams(vmem_limit_bytes=60 << 20),
        name="hand_over",
    )(*found)


def hand_over(*refs):
    given, wanted, held, (inward, outward) = refs[:5], refs[5:10], refs[10:15], refs[15:]
    first = [pltpu.make_async_copy(given[n], held[n], inward.at[n]) for n in range(5)]
    last = [pltpu.make_async_copy(held[n], wanted[n], outward.at[n]) for n in range(5)]
    for copy in first:
        copy.start()
    for n in range(5):
        first[n].wait()
        last[n].start()
    for copy in last:
        copy.wait()


def solution(mesh):
    split = P(None, ("row", "col"))
    listed = P(("row", "col"))
    return jax.shard_map(
        lambda *args: tuple(body(*args)),
        mesh=mesh,
        in_specs=(split,) * 6 + (listed,) * 3 + (P(),),
        out_specs=(split,) * 4 + (P(),),
        check_vma=False,
    )
```

```python
import functools

import jax
import jax.numpy as jnp
from jax import lax
from jax.experimental import pallas as pl
from jax.experimental.pallas import tpu as pltpu
from jax.sharding import PartitionSpec as P

F32 = jnp.float32
I32 = jnp.int32
BF16 = jnp.bfloat16
MESH = pl.DeviceIdType.MESH
DMA = pltpu.SemaphoreType.DMA

MODES, TILE, BPD, SLOTS = 64, 64, 16, 576
NROW, NCOL = 32, 8
LOCAL = TILE * BPD
DOFS = LOCAL * NROW * NCOL
PLANE, DEEP = 8, 4
SIZES = {"xc": PLANE, "y": DEEP, "z": NCOL}
LANES = 128
STRIPS = LOCAL // LANES
BLOCKS = NCOL * BPD
ROWS = 3 * BPD
PARTS = 4
HOPS = 3 * PARTS + PARTS // 2
PER = STRIPS // PARTS
RANKS = 640
PAIRS = SLOTS // 2 + ROWS // 2
BATCH = 24
FRESH = 1 << 18


def halves(value):
    high = value.astype(BF16)
    return high, (value - high.astype(F32)).astype(BF16)


def product(a, b, dims):
    dot = functools.partial(
        lax.dot_general, dimension_numbers=(dims, ((), ())), preferred_element_type=F32
    )
    a_high, a_low = halves(a)
    b_high, b_low = halves(b)
    return dot(a_high, b_high) + (dot(a_high, b_low) + dot(a_low, b_high))


NN = ((1,), (0,))
NT = ((1,), (1,))
TN = ((0,), (0,))


class Place:
    def __init__(self):
        i, j = lax.axis_index("row"), lax.axis_index("col")
        self.i, self.j = i, j
        plane, inner = i // PLANE, lax.rem(i, PLANE)
        self.groups = {
            "xc": (PLANE, inner, lambda m: (plane * PLANE + m, j)),
            "y": (DEEP, plane, lambda m: (m * PLANE + inner, j)),
            "z": (NCOL, j, lambda m: (i, m)),
        }
        self.next_row = (lax.rem(i + 1, NROW), j)
        self.last_row = (lax.rem(i + NROW - 1, NROW), j)
        self.right = (i, lax.rem(j + 1, NCOL))
        self.left = (i, lax.rem(j + NCOL - 1, NCOL))


def greet(place, rows):
    barrier = pltpu.get_barrier_semaphore()
    devices = [place.next_row, place.last_row] if rows else []
    for size, me, device in place.groups.values():
        devices += [device(lax.rem(me + o, size)) for o in range(1, size)]
    for device in devices:
        pl.semaphore_signal(barrier, inc=1, device_id=device, device_id_type=MESH)
    return lambda: pl.semaphore_wait(barrier, len(devices))


def swap(place, name, source, landing, sends, recvs):
    size, me, device = place.groups[name]
    copies = []
    for o in range(1, size):
        peer = lax.rem(me + o, size)
        copy = pltpu.make_async_remote_copy(
            src_ref=source(peer),
            dst_ref=landing.at[me],
            send_sem=sends.at[o],
            recv_sem=recvs.at[o],
            device_id=device(peer),
            device_id_type=MESH,
        )
        copy.start()
        copies.append(copy)
    return copies


def finish(copies):
    for copy in copies:
        copy.wait()


def total(landing):
    value = landing[0]
    for m in range(1, landing.shape[0]):
        value = value + landing[m]
    return value


class Scratch:
    def __init__(self, shapes):
        self.names, self.shapes = list(shapes), list(shapes.values())

    def found(self, refs):
        return dict(zip(self.names, refs))


def sum_theta(place, local, refs, tag, work):
    value = jnp.concatenate([local[:32], local[32:]], axis=1)
    for at, name in enumerate(SIZES):
        landing = refs[f"{tag}_{name}"]
        me = place.groups[name][1]
        landing[me] = value
        copies = swap(
            place,
            name,
            lambda peer: landing.at[me],
            landing,
            refs[f"{tag}_{name}_s"],
            refs[f"{tag}_{name}_r"],
        )
        work[at]()
        finish(copies)
        value = total(landing)
    return jnp.concatenate([value[:, :64], value[:, 64:]], axis=0)


def theta_scratch(tag):
    shapes = {}
    for name, size in SIZES.items():
        shapes[f"{tag}_{name}"] = pltpu.VMEM((size, 32, LANES), F32)
        shapes[f"{tag}_{name}_s"] = DMA((size,))
        shapes[f"{tag}_{name}_r"] = DMA((size,))
    return shapes


STAGES = ("xc", "y", "z", "y", "xc")


def mix_scratch(tag, rows):
    r = rows // NROW
    big, mid = (PLANE, DEEP, r, LANES), (DEEP, r, LANES)
    shapes = {
        f"{tag}_{n}": pltpu.VMEM(s, F32)
        for n, s in enumerate((big, big, mid, mid, (NCOL, r, LANES), mid, big))
    }
    for n, name in enumerate(STAGES):
        shapes[f"{tag}_s{n}"] = DMA((SIZES[name],))
        shapes[f"{tag}_r{n}"] = DMA((SIZES[name],))
    return shapes


def mix(place, rows, flat, refs, tag):
    r = rows // NROW
    data, land_a, half, land_b, land_z, back, result = (refs[f"{tag}_{n}"] for n in range(7))
    sems = [(refs[f"{tag}_s{n}"], refs[f"{tag}_r{n}"]) for n in range(5)]
    mine = {name: place.groups[name][1] for name in SIZES}
    for a in range(PLANE):
        for b in range(DEEP):
            at = (a * DEEP + b) * r
            data[a, b] = flat[at : at + r, :]
    land_a[mine["xc"]] = data[mine["xc"]]
    copies = swap(place, "xc", lambda peer: data.at[peer], land_a, *sems[0])
    yield
    finish(copies)
    half[...] = total(land_a)
    land_b[mine["y"]] = half[mine["y"]]
    copies = swap(place, "y", lambda peer: half.at[peer], land_b, *sems[1])
    yield
    finish(copies)
    land_z[mine["z"]] = total(land_b)
    copies = swap(place, "z", lambda peer: land_z.at[mine["z"]], land_z, *sems[2])
    yield
    finish(copies)
    back[mine["y"]] = total(land_z)
    copies = swap(place, "y", lambda peer: back.at[mine["y"]], back, *sems[3])
    yield
    finish(copies)
    result[mine["xc"]] = back[...]
    copies = swap(place, "xc", lambda peer: result.at[mine["xc"]], result, *sems[4])
    yield
    finish(copies)
    for a in range(PLANE):
        for b in range(DEEP):
            at = (a * DEEP + b) * r
            flat[at : at + r, :] = result[a, b]
    yield


def short_scratch(tag, rows):
    r = rows // PLANE
    shapes = {
        f"{tag}_{n}": pltpu.VMEM((size, r, LANES), F32)
        for n, size in enumerate((PLANE, PLANE, DEEP, NCOL, PLANE))
    }
    for n, name in enumerate(("xc", "y", "z", "xc")):
        shapes[f"{tag}_s{n}"] = DMA((SIZES[name],))
        shapes[f"{tag}_r{n}"] = DMA((SIZES[name],))
    return shapes


def mix_short(place, rows, flat, refs, tag):
    r = rows // PLANE
    data, land_a, land_b, land_z, result = (refs[f"{tag}_{n}"] for n in range(5))
    sems = [(refs[f"{tag}_s{n}"], refs[f"{tag}_r{n}"]) for n in range(4)]
    mine = {name: place.groups[name][1] for name in SIZES}
    for a in range(PLANE):
        data[a] = flat[a * r : (a + 1) * r, :]
    land_a[mine["xc"]] = data[mine["xc"]]
    copies = swap(place, "xc", lambda peer: data.at[peer], land_a, *sems[0])
    yield
    finish(copies)
    land_b[mine["y"]] = total(land_a)
    copies = swap(place, "y", lambda peer: land_b.at[mine["y"]], land_b, *sems[1])
    yield
    finish(copies)
    land_z[mine["z"]] = total(land_b)
    copies = swap(place, "z", lambda peer: land_z.at[mine["z"]], land_z, *sems[2])
    yield
    finish(copies)
    result[mine["xc"]] = total(land_z)
    copies = swap(place, "xc", lambda peer: result.at[mine["xc"]], result, *sems[3])
    yield
    finish(copies)
    for a in range(PLANE):
        flat[a * r : (a + 1) * r, :] = result[a]
    yield


def ring_scratch(tag):
    return {
        f"{tag}_held": pltpu.VMEM((NCOL, STRIPS, MODES, LANES), F32),
        f"{tag}_s": DMA((2, HOPS)),
        f"{tag}_r": DMA((2, HOPS)),
    }


class Ring:
    def __init__(self, place, refs, tag, spread_ref):
        self.place, self.spread_ref = place, spread_ref
        self.held, self.sends, self.recvs = (refs[f"{tag}_{n}"] for n in ("held", "s", "r"))
        self.devices = (place.right, place.left)

    def region(self, way, n, hop):
        q, s = n // PARTS, lax.rem(n, PARTS)
        if way == 0:
            return lax.rem(self.place.j + 2 * NCOL - q - hop, NCOL), s
        return lax.rem(self.place.j + q + hop, NCOL), lax.rem(s + PARTS // 2, PARTS)

    def copy(self, way, n, hop=0):
        slot, part = self.region(way, n, hop)
        piece = self.held.at[slot, pl.ds(part * PER, PER)]
        return pltpu.make_async_remote_copy(
            src_ref=piece,
            dst_ref=piece,
            send_sem=self.sends.at[way, n],
            recv_sem=self.recvs.at[way, n],
            device_id=self.devices[way],
            device_id_type=MESH,
        )

    def spread(self, slot, first, count):
        def one(b, carry):
            value = self.held[slot, first + b]
            high = value.astype(BF16).astype(F32)
            at = 2 * (slot * STRIPS + first + b) + 1
            both = jnp.concatenate([high, value - high], axis=0).T.astype(BF16)
            self.spread_ref[at] = both[:TILE]
            self.spread_ref[at + 1] = both[TILE:]
            return carry

        lax.fori_loop(0, count, one, 0)

    def run(self, tasks, each):
        def step(n, carry):
            for way in range(2):
                self.copy(way, n, 1).wait_recv()

                @pl.when(n + PARTS < HOPS)
                def forward():
                    self.copy(way, n + PARTS).start()

            for way in range(2):
                slot, part = self.region(way, n, 1)
                self.spread(slot, part * PER, PER)
            each(n)
            return carry

        def end(n, carry):
            for way in range(2):
                self.copy(way, n).wait_send()
            return carry

        done = 0
        for stop, task in tasks:
            lax.fori_loop(done, stop, step, 0)
            task()
            done = stop
        lax.fori_loop(done, HOPS, step, 0)
        lax.fori_loop(0, HOPS, end, 0)


def line(ref):
    value = ref[...].reshape(1, SLOTS)
    return jnp.concatenate([value, jnp.zeros((1, RANKS - SLOTS), I32)], axis=1)


def upright(value):
    return jnp.broadcast_to(value, (LANES, RANKS)).T


def count_of(where, value=1):
    return jnp.sum(jnp.where(where, value, 0), axis=0, keepdims=True)


def order(rows, cols, live):
    lane = lax.broadcasted_iota(I32, (1, RANKS), 1)
    row = jnp.where(lane < live, rows, 255)
    below = lax.broadcasted_iota(I32, (RANKS, LANES), 0)
    row_up = upright(row)
    rank = []
    for b in range(RANKS // LANES):
        here = lax.broadcasted_iota(I32, (RANKS, LANES), 1) + b * LANES
        same = (row_up == row[:, b * LANES : (b + 1) * LANES]) & (below < here)
        rank.append(count_of(same))
    rank = jnp.concatenate(rank, axis=1)
    name = lax.broadcasted_iota(I32, (RANKS, LANES), 1)
    held = count_of(row_up == name)
    pairs = jnp.right_shift(held + 1, 1)
    pairs_up = jnp.broadcast_to(pairs, (LANES, LANES)).T[:ROWS]
    named = lax.broadcasted_iota(I32, (ROWS, RANKS), 0)
    wide_pairs = jnp.concatenate([pairs_up] * (RANKS // LANES), axis=1)
    start = count_of(named < row, wide_pairs)
    place = jnp.where(lane < live, 2 * start + rank, 5000)
    code = lane + 1024 * (cols + 1) + jnp.where(rank == 0, FRESH, 0)
    place_up, code_up = upright(place), upright(code)
    found = []
    for b in range(RANKS // LANES):
        here = lax.broadcasted_iota(I32, (RANKS, LANES), 1) + b * LANES
        found.append(count_of(place_up == here, code_up))
    mine = lax.broadcasted_iota(I32, (ROWS, LANES), 0)
    at = lax.broadcasted_iota(I32, (ROWS, LANES), 1)
    ends = jnp.where(pairs > 0, count_of(mine <= at, pairs_up), 0)
    return jnp.concatenate(found, axis=1), ends


def pack_pair(p, codes, tiles, packed):
    half = jnp.right_shift(lax.broadcasted_iota(I32, (TILE, LANES), 1), 6)

    def one(place, wanted):
        slot = jnp.bitwise_and(codes[0, place], 1023)
        value = tiles[:, pl.ds(jnp.right_shift(slot, 1) * LANES, LANES)]
        odd = jnp.broadcast_to(jnp.bitwise_and(slot, 1), (TILE, LANES))
        return jnp.where(odd == wanted, value, pltpu.roll(value, TILE, 1))

    both = jnp.where(half == 0, one(2 * p, 0), one(2 * p + 1, 1))
    packed[p] = jnp.concatenate(halves(both), axis=1)


def multiply(codes, ends, packed, spread_ref, sums, part, after):
    def batch(s, run):
        found = []
        for u in range(BATCH):
            p = s * BATCH + u
            pair = (codes[0, 2 * p], codes[0, 2 * p + 1])
            tables = []
            for code in pair:
                tables.append(spread_ref[jnp.bitwise_and(jnp.right_shift(code, 10), 255)])
            out = jnp.dot(
                packed[p], jnp.concatenate(tables * 2, axis=0), preferred_element_type=F32
            )
            fresh = jnp.broadcast_to(pair[0], (TILE, LANES)) >= FRESH
            found.append((p, fresh, out))
        for p, fresh, out in found:
            run = jnp.where(fresh, 0.0, run) + out
            sums[p + 1] = run
        return run

    sums[0] = jnp.zeros((TILE, LANES), F32)
    lax.fori_loop(0, PAIRS // BATCH, batch, jnp.zeros((TILE, LANES), F32))

    def place(b, carry):
        both = jnp.concatenate([sums[ends[0, 2 * b]], sums[ends[0, 2 * b + 1]]], axis=0).T
        part[:, pl.ds(pl.multiple_of(b * LANES, LANES), LANES)] = both[:MODES] + both[MODES:]
        return carry

    for third in (0, 2, 1):
        lax.fori_loop(third * STRIPS, (third + 1) * STRIPS, place, 0)
        after(third)


def correct(place, x, ax, diag, theta_t, w, ring):
    for part, way, n in ((0, 0, 0), (2, 1, 0), (1, 0, 1), (3, 1, 1)):
        for s in range(part * PER, (part + 1) * PER):
            at = slice(s * LANES, (s + 1) * LANES)
            value = (ax[:, at] - product(theta_t, x[:, at], NN)) / diag[:, at]
            w[:, at] = value
            ring.held[place.j, s] = value
        ring.copy(way, n).start()
    for n in (2, 3):
        for way in range(2):
            ring.copy(way, n).start()


def theta_local(x, ax):
    return product(ax[...], x[...], NT) * (1.0 / DOFS)


def fold(value):
    return jnp.concatenate([value[:96], value[96:]], axis=1)


def unfold(value):
    return jnp.concatenate([value[:, :64], value[:, 64:]], axis=0)


def gram_rest(x, w, p, ax, ap, flat, base):
    basis = jnp.concatenate([x[...], w[...], p[...]], axis=0)
    other = jnp.concatenate([ax[...], ap[...], basis], axis=0)
    block = product(basis, other, NT) * (1.0 / DOFS)
    flat[base : base + 192, :] = block[:, :128]
    flat[base + 192 : base + 384, :] = block[:, 128:256]
    flat[base + 384 : base + 480, :] = fold(block[:, 256:])


def gram_image(x, w, p, aw, flat):
    basis = jnp.concatenate([x[...], w[...], p[...]], axis=0)
    flat[0:96, :] = fold(product(basis, aw[...], NT) * (1.0 / DOFS))


def halo_scratch(tag):
    return {
        f"{tag}_above": pltpu.VMEM((MODES, LOCAL), F32),
        f"{tag}_below": pltpu.VMEM((MODES, LOCAL), F32),
        f"{tag}_s": DMA((2,)),
        f"{tag}_r": DMA((2,)),
    }


def halo(place, part, refs, tag, third):
    at = third // 2
    copy = pltpu.make_async_remote_copy(
        src_ref=part.at[:, pl.ds(third * LOCAL, LOCAL)],
        dst_ref=refs[f"{tag}_below" if at else f"{tag}_above"],
        send_sem=refs[f"{tag}_s"].at[at],
        recv_sem=refs[f"{tag}_r"].at[at],
        device_id=place.next_row if at else place.last_row,
        device_id_type=MESH,
    )
    copy.start()
    return copy


def near_scratch():
    shapes = {f"near_{n}": pltpu.VMEM((2, MODES, LOCAL), F32) for n in "xpw"}
    return shapes | {"near_s": DMA((6,)), "near_r": DMA((6,))}


def lend(place, refs, name, field):
    copies = []
    for side, device in enumerate((place.next_row, place.last_row)):
        at = 2 * "xpw".index(name) + side
        copy = pltpu.make_async_remote_copy(
            src_ref=field,
            dst_ref=refs[f"near_{name}"].at[side],
            send_sem=refs["near_s"].at[at],
            recv_sem=refs["near_r"].at[at],
            device_id=device,
            device_id_type=MESH,
        )
        copy.start()
        copies.append(copy)
    return copies


def image(part, w, diag, refs, tag, aw):
    aw[...] = (
        part[:, LOCAL : 2 * LOCAL]
        + refs[f"{tag}_below"][...]
        + refs[f"{tag}_above"][...]
        + diag[...] * w[...]
    )


def rotate(turn, x, w, p, next_x, next_p):
    moved = product(turn[:, 64:], jnp.concatenate([w[...], p[...]], axis=0), NN)
    next_p[...] = moved
    next_x[...] = product(turn[:, :64], x[...], NN) + moved


def put_grams(rest, image_block, grams, k):
    block = rest[0:192]
    grams[k, 0] = jnp.concatenate([block[:, :64], unfold(image_block), block[:, 64:]], axis=1)
    grams[k, 1] = jnp.concatenate([rest[192:384], unfold(rest[384:480])], axis=1)


FIELDS = ("x", "ax", "diag", "p", "ap")
FIELD = pltpu.VMEM((MODES, LOCAL), F32)
NAMED = Scratch(
    {name: FIELD for name in FIELDS}
    | {f"{n}{k}": FIELD for k in (1, 2) for n in ("x", "p", "ax", "ap")}
    | {name: FIELD for name in ("w", "w1", "aw", "aw1")}
    | {
        "turn": pltpu.VMEM((2, MODES, 3 * MODES), F32),
        "tiles": pltpu.VMEM((TILE, SLOTS * TILE), F32),
        "loads": DMA((7,)),
        "stores": DMA((6,)),
        "codes_v": pltpu.VMEM((1, RANKS), I32),
        "ends_v": pltpu.VMEM((1, LANES), I32),
        "codes": pltpu.SMEM((1, RANKS), I32),
        "ends": pltpu.SMEM((1, LANES), I32),
        "lists": DMA((2,)),
        "packed": pltpu.VMEM((PAIRS, TILE, 2 * LANES), BF16),
        "sums": pltpu.VMEM((PAIRS + 1, TILE, LANES), F32),
        "spread": pltpu.VMEM((BLOCKS + 1, TILE, LANES), BF16),
        "part": pltpu.VMEM((MODES, 3 * LOCAL), F32),
        "flat0": pltpu.VMEM((480, LANES), F32),
        "flat1": pltpu.VMEM((576, LANES), F32),
        "flat2": pltpu.VMEM((96, LANES), F32),
        "grams": pltpu.VMEM((2, 2, 192, 192), F32),
    }
    | {"before_t": pltpu.VMEM((MODES, MODES), F32), "before_g": pltpu.VMEM((192, MODES), F32)}
    | near_scratch()
    | theta_scratch("theta0")
    | theta_scratch("theta1")
    | ring_scratch("ring0")
    | ring_scratch("ring1")
    | halo_scratch("halo0")
    | halo_scratch("halo1")
    | mix_scratch("mix0", 480)
    | mix_scratch("mix1", 576)
    | short_scratch("mix2", 96)
)
BESIDE_Y, BESIDE_Z = 72, 200


def steps(
    rows, cols, count, x_in, ax_in, diag_in, p_in, ap_in, turn_in, tiles_in,
    x_out, p_out, ax_out, ap_out, grams_out, *refs,
):
    place = Place()
    ready = greet(place, rows=True)
    r = NAMED.found(refs)
    loads = {}
    for n, (name, source) in enumerate(
        zip(FIELDS + ("turn", "tiles"), (x_in, ax_in, diag_in, p_in, ap_in, turn_in, tiles_in))
    ):
        loads[name] = pltpu.make_async_copy(source, r[name], r["loads"].at[n])
        loads[name].start()
    stores = []

    def store(source, target):
        copy = pltpu.make_async_copy(source, target, r["stores"].at[len(stores)])
        copy.start()
        stores.append(copy)

    codes, ends, packed, tiles = r["codes"], r["ends"], r["packed"], r["tiles"]
    x, ax, diag, p, ap = (r[name] for name in FIELDS)
    w, w1, aw, aw1, part, spread_ref = (
        r[n] for n in ("w", "w1", "aw", "aw1", "part", "spread")
    )

    def nothing(*unused):
        pass

    def sort():
        code, end = order(line(rows), line(cols), count[0])
        r["codes_v"][...] = code
        r["ends_v"][...] = end
        moves = [
            pltpu.make_async_copy(r["codes_v"], codes, r["lists"].at[0]),
            pltpu.make_async_copy(r["ends_v"], ends, r["lists"].at[1]),
        ]
        for move in moves:
            move.start()
        for move in moves:
            move.wait()
        spread_ref[0] = jnp.zeros((TILE, LANES), BF16)

    def pack(a, b):
        def four(s, carry):
            for u in range(4):
                pack_pair(4 * s + u, codes, tiles, packed)
            return carry

        return lambda: lax.fori_loop(a // 4, b // 4, four, 0)

    def pack_first():
        loads["tiles"].wait()
        pack(0, BESIDE_Y)()

    loads["x"].wait()
    loads["ax"].wait()
    local = theta_local(x, ax)
    ready()
    theta_t = sum_theta(
        place, local, r, "theta0", (sort, pack_first, pack(BESIDE_Y, BESIDE_Z))
    )
    loads["diag"].wait()
    ring = Ring(place, r, "ring0", spread_ref)
    correct(place, x, ax, diag, theta_t, w, ring)
    loads["p"].wait()
    loads["ap"].wait()
    loads["turn"].wait()
    flat0, flat1, flat2, before_t, before_g = (
        r[n] for n in ("flat0", "flat1", "flat2", "before_t", "before_g")
    )
    x1, p1, ax1, ap1 = (r[n] for n in ("x1", "p1", "ax1", "ap1"))
    x2, p2, ax2, ap2 = (r[n] for n in ("x2", "p2", "ax2", "ap2"))
    near_x, near_p, near_w = (r[f"near_{n}"] for n in "xpw")
    mix0 = mix(place, 480, flat0, r, "mix0")
    mix1 = mix(place, 576, flat1, r, "mix1")
    mix2 = mix_short(place, 96, flat2, r, "mix2")
    lent, sent = [], []

    def thirds(n):
        return part[:, n * LOCAL : (n + 1) * LOCAL]

    def own0():
        ring.spread(place.j, 0, STRIPS)
        gram_rest(x, w, p, ax, ap, flat0, 0)
        next(mix0)

    def turn0():
        rotate(r["turn"][0], x, w, p, x1, p1)
        lent.extend(lend(place, r, "x", x1))
        lent.extend(lend(place, r, "p", p1))

    def theta0():
        known = jnp.concatenate([ax[...], diag[...] * w[...], ap[...]], axis=0)
        before_t[...] = product(product(r["turn"][0], known, NN), x1[...], NT)

    def each0(n):
        for u in range(8):
            pack_pair(BESIDE_Z + n * 8 + u, codes, tiles, packed)

    def send(tag):
        return lambda third: third == 1 or sent.append(halo(place, part, r, tag, third))

    ring.run(((0, own0), (3, turn0), (6, lambda: next(mix0)), (8, theta0)), each0)
    next(mix0)
    multiply(codes, ends, packed, spread_ref, r["sums"], part, send("halo0"))
    next(mix0)
    finish(lent)
    core = (
        product(thirds(0), near_x[0], NT)
        + product(thirds(2), near_x[1], NT)
        + product(thirds(1), x1[...], NT)
    )
    local = before_t[...] + product(r["turn"][0][:, 64:128], core, NN)

    def images0():
        finish(sent)
        image(part, w, diag, r, "halo0", aw)
        rotate(r["turn"][0], ax, aw, ap, ax1, ap1)

    def grams0():
        gram_image(x, w, p, aw, flat1)

    theta_t = sum_theta(
        place, local * (1.0 / DOFS), r, "theta1", (nothing, images0, grams0)
    )
    ring = Ring(place, r, "ring1", spread_ref)
    correct(place, x1, ax1, diag, theta_t, w1, ring)
    lent, sent = [], []

    def own1():
        lent.extend(lend(place, r, "w", w1))
        ring.spread(place.j, 0, STRIPS)
        gram_rest(x1, w1, p1, ax1, ap1, flat1, 96)
        next(mix1)

    def turn1():
        rotate(r["turn"][1], x1, w1, p1, x2, p2)
        store(x2, x_out)
        store(p2, p_out)

    def image1():
        basis = jnp.concatenate([x1[...], w1[...], p1[...]], axis=0)
        before_g[...] = product(basis, diag[...] * w1[...], NT)

    def both():
        next(mix0)
        next(mix1)

    ring.run(
        ((0, own1), (3, turn1), (5, lambda: next(mix0)), (7, image1), (9, both)), nothing
    )
    next(mix1)
    multiply(codes, ends, packed, spread_ref, r["sums"], part, send("halo1"))
    next(mix1)
    finish(lent)
    total_image = before_g[...]
    for third, fields in (
        (0, (near_x[0], near_w[0], near_p[0])),
        (1, (x1[...], w1[...], p1[...])),
        (2, (near_x[1], near_w[1], near_p[1])),
    ):
        total_image += product(jnp.concatenate(fields, axis=0), thirds(third), NT)
    flat2[...] = fold(total_image * (1.0 / DOFS))
    next(mix2)
    next(mix2)
    finish(sent)
    image(part, w1, diag, r, "halo1", aw1)
    next(mix2)
    next(mix1)
    rotate(r["turn"][1], ax1, aw1, ap1, ax2, ap2)
    store(ax2, ax_out)
    store(ap2, ap_out)
    next(mix1)
    put_grams(flat0[...], flat1[0:96], r["grams"], 0)
    store(r["grams"].at[0], grams_out.at[0])
    next(mix2)
    next(mix2)
    put_grams(flat1[96:576], flat2[...], r["grams"], 1)
    store(r["grams"].at[1], grams_out.at[1])
    for copy in stores:
        copy.wait()


def body(x, p, ax, ap, diag, tiles, rows, cols, count, turns):
    field = jax.ShapeDtypeStruct((MODES, LOCAL), F32)
    far = pl.BlockSpec(memory_space=pl.ANY)
    found = pl.pallas_call(
        steps,
        out_shape=[field] * 4 + [jax.ShapeDtypeStruct((2, 2, 192, 192), F32)],
        in_specs=[
            pl.BlockSpec(memory_space=pltpu.VMEM),
            pl.BlockSpec(memory_space=pltpu.VMEM),
            pl.BlockSpec(memory_space=pltpu.SMEM),
        ]
        + [far] * 7,
        out_specs=[far] * 5,
        scratch_shapes=NAMED.shapes,
        compiler_params=pltpu.CompilerParams(
            collective_id=1, has_side_effects=True, vmem_limit_bytes=60 << 20
        ),
        name="steps",
    )(rows, cols, count, x, ax, diag, p, ap, turns.swapaxes(1, 2), tiles)
    return pl.pallas_call(
        hand_over,
        out_shape=[jax.ShapeDtypeStruct(f.shape, f.dtype) for f in found],
        in_specs=[far] * 5,
        out_specs=[far] * 5,
        scratch_shapes=[pltpu.VMEM(f.shape, f.dtype) for f in found] + [DMA((5,))] * 2,
        compiler_params=pltpu.CompilerParams(vmem_limit_bytes=60 << 20),
        name="hand_over",
    )(*found)


def hand_over(*refs):
    given, wanted, held, (inward, outward) = refs[:5], refs[5:10], refs[10:15], refs[15:]
    first = [pltpu.make_async_copy(given[n], held[n], inward.at[n]) for n in range(5)]
    last = [pltpu.make_async_copy(held[n], wanted[n], outward.at[n]) for n in range(5)]
    for copy in first:
        copy.start()
    for n in range(5):
        first[n].wait()
        last[n].start()
    for copy in last:
        copy.wait()


def solution(mesh):
    split = P(None, ("row", "col"))
    listed = P(("row", "col"))
    return jax.shard_map(
        lambda *args: tuple(body(*args)),
        mesh=mesh,
        in_specs=(split,) * 6 + (listed,) * 3 + (P(),),
        out_specs=(split,) * 4 + (P(),),
        check_vma=False,
    )
```

```python
import functools

import jax
import jax.numpy as jnp
from jax import lax
from jax.experimental import pallas as pl
from jax.experimental.pallas import tpu as pltpu
from jax.sharding import PartitionSpec as P

F32 = jnp.float32
I32 = jnp.int32
BF16 = jnp.bfloat16
MESH = pl.DeviceIdType.MESH
DMA = pltpu.SemaphoreType.DMA

MODES, TILE, BPD, SLOTS = 64, 64, 16, 576
NROW, NCOL = 32, 8
LOCAL = TILE * BPD
DOFS = LOCAL * NROW * NCOL
PLANE, DEEP = 8, 4
SIZES = {"xc": PLANE, "y": DEEP, "z": NCOL}
LANES = 128
STRIPS = LOCAL // LANES
BLOCKS = NCOL * BPD
ROWS = 3 * BPD
PARTS = 4
HOPS = 3 * PARTS + PARTS // 2
PER = STRIPS // PARTS
RANKS = 640
PAIRS = SLOTS // 2 + ROWS // 2
BATCH = 78
FRESH = 1 << 18


def halves(value):
    high = value.astype(BF16)
    return high, (value - high.astype(F32)).astype(BF16)


def product(a, b, dims):
    dot = functools.partial(
        lax.dot_general, dimension_numbers=(dims, ((), ())), preferred_element_type=F32
    )
    a_high, a_low = halves(a)
    b_high, b_low = halves(b)
    return dot(a_high, b_high) + (dot(a_high, b_low) + dot(a_low, b_high))


NN = ((1,), (0,))
NT = ((1,), (1,))
TN = ((0,), (0,))


class Place:
    def __init__(self):
        i, j = lax.axis_index("row"), lax.axis_index("col")
        self.i, self.j = i, j
        plane, inner = i // PLANE, lax.rem(i, PLANE)
        self.groups = {
            "xc": (PLANE, inner, lambda m: (plane * PLANE + m, j)),
            "y": (DEEP, plane, lambda m: (m * PLANE + inner, j)),
            "z": (NCOL, j, lambda m: (i, m)),
        }
        self.next_row = (lax.rem(i + 1, NROW), j)
        self.last_row = (lax.rem(i + NROW - 1, NROW), j)
        self.right = (i, lax.rem(j + 1, NCOL))
        self.left = (i, lax.rem(j + NCOL - 1, NCOL))


def greet(place, rows):
    barrier = pltpu.get_barrier_semaphore()
    devices = [place.next_row, place.last_row] if rows else []
    for size, me, device in place.groups.values():
        devices += [device(lax.rem(me + o, size)) for o in range(1, size)]
    for device in devices:
        pl.semaphore_signal(barrier, inc=1, device_id=device, device_id_type=MESH)
    return lambda: pl.semaphore_wait(barrier, len(devices))


def swap(place, name, source, landing, sends, recvs):
    size, me, device = place.groups[name]
    copies = []
    for o in range(1, size):
        peer = lax.rem(me + o, size)
        copy = pltpu.make_async_remote_copy(
            src_ref=source(peer),
            dst_ref=landing.at[me],
            send_sem=sends.at[o],
            recv_sem=recvs.at[o],
            device_id=device(peer),
            device_id_type=MESH,
        )
        copy.start()
        copies.append(copy)
    return copies


def finish(copies):
    for copy in copies:
        copy.wait()


def total(landing):
    value = landing[0]
    for m in range(1, landing.shape[0]):
        value = value + landing[m]
    return value


class Scratch:
    def __init__(self, shapes):
        self.names, self.shapes = list(shapes), list(shapes.values())

    def found(self, refs):
        return dict(zip(self.names, refs))


def sum_theta(place, local, refs, tag, work):
    value = jnp.concatenate([local[:32], local[32:]], axis=1)
    for at, name in enumerate(SIZES):
        landing = refs[f"{tag}_{name}"]
        me = place.groups[name][1]
        landing[me] = value
        copies = swap(
            place,
            name,
            lambda peer: landing.at[me],
            landing,
            refs[f"{tag}_{name}_s"],
            refs[f"{tag}_{name}_r"],
        )
        work[at]()
        finish(copies)
        value = total(landing)
    return jnp.concatenate([value[:, :64], value[:, 64:]], axis=0)


def theta_scratch(tag):
    shapes = {}
    for name, size in SIZES.items():
        shapes[f"{tag}_{name}"] = pltpu.VMEM((size, 32, LANES), F32)
        shapes[f"{tag}_{name}_s"] = DMA((size,))
        shapes[f"{tag}_{name}_r"] = DMA((size,))
    return shapes


STAGES = ("xc", "y", "z", "y", "xc")


def mix_scratch(tag, rows):
    r = rows // NROW
    big, mid = (PLANE, DEEP, r, LANES), (DEEP, r, LANES)
    shapes = {
        f"{tag}_{n}": pltpu.VMEM(s, F32)
        for n, s in enumerate((big, big, mid, mid, (NCOL, r, LANES), mid, big))
    }
    for n, name in enumerate(STAGES):
        shapes[f"{tag}_s{n}"] = DMA((SIZES[name],))
        shapes[f"{tag}_r{n}"] = DMA((SIZES[name],))
    return shapes


def mix(place, rows, flat, refs, tag):
    r = rows // NROW
    data, land_a, half, land_b, land_z, back, result = (refs[f"{tag}_{n}"] for n in range(7))
    sems = [(refs[f"{tag}_s{n}"], refs[f"{tag}_r{n}"]) for n in range(5)]
    mine = {name: place.groups[name][1] for name in SIZES}
    for a in range(PLANE):
        for b in range(DEEP):
            at = (a * DEEP + b) * r
            data[a, b] = flat[at : at + r, :]
    land_a[mine["xc"]] = data[mine["xc"]]
    copies = swap(place, "xc", lambda peer: data.at[peer], land_a, *sems[0])
    yield
    finish(copies)
    half[...] = total(land_a)
    land_b[mine["y"]] = half[mine["y"]]
    copies = swap(place, "y", lambda peer: half.at[peer], land_b, *sems[1])
    yield
    finish(copies)
    land_z[mine["z"]] = total(land_b)
    copies = swap(place, "z", lambda peer: land_z.at[mine["z"]], land_z, *sems[2])
    yield
    finish(copies)
    back[mine["y"]] = total(land_z)
    copies = swap(place, "y", lambda peer: back.at[mine["y"]], back, *sems[3])
    yield
    finish(copies)
    result[mine["xc"]] = back[...]
    copies = swap(place, "xc", lambda peer: result.at[mine["xc"]], result, *sems[4])
    yield
    finish(copies)
    for a in range(PLANE):
        for b in range(DEEP):
            at = (a * DEEP + b) * r
            flat[at : at + r, :] = result[a, b]
    yield


def short_scratch(tag, rows):
    r = rows // PLANE
    shapes = {
        f"{tag}_{n}": pltpu.VMEM((size, r, LANES), F32)
        for n, size in enumerate((PLANE, PLANE, DEEP, NCOL, PLANE))
    }
    for n, name in enumerate(("xc", "y", "z", "xc")):
        shapes[f"{tag}_s{n}"] = DMA((SIZES[name],))
        shapes[f"{tag}_r{n}"] = DMA((SIZES[name],))
    return shapes


def mix_short(place, rows, flat, refs, tag):
    r = rows // PLANE
    data, land_a, land_b, land_z, result = (refs[f"{tag}_{n}"] for n in range(5))
    sems = [(refs[f"{tag}_s{n}"], refs[f"{tag}_r{n}"]) for n in range(4)]
    mine = {name: place.groups[name][1] for name in SIZES}
    for a in range(PLANE):
        data[a] = flat[a * r : (a + 1) * r, :]
    land_a[mine["xc"]] = data[mine["xc"]]
    copies = swap(place, "xc", lambda peer: data.at[peer], land_a, *sems[0])
    yield
    finish(copies)
    land_b[mine["y"]] = total(land_a)
    copies = swap(place, "y", lambda peer: land_b.at[mine["y"]], land_b, *sems[1])
    yield
    finish(copies)
    land_z[mine["z"]] = total(land_b)
    copies = swap(place, "z", lambda peer: land_z.at[mine["z"]], land_z, *sems[2])
    yield
    finish(copies)
    result[mine["xc"]] = total(land_z)
    copies = swap(place, "xc", lambda peer: result.at[mine["xc"]], result, *sems[3])
    yield
    finish(copies)
    for a in range(PLANE):
        flat[a * r : (a + 1) * r, :] = result[a]
    yield


def ring_scratch(tag):
    return {
        f"{tag}_held": pltpu.VMEM((NCOL, STRIPS, MODES, LANES), F32),
        f"{tag}_s": DMA((2, HOPS)),
        f"{tag}_r": DMA((2, HOPS)),
    }


class Ring:
    def __init__(self, place, refs, tag, spread_ref):
        self.place, self.spread_ref = place, spread_ref
        self.held, self.sends, self.recvs = (refs[f"{tag}_{n}"] for n in ("held", "s", "r"))
        self.devices = (place.right, place.left)

    def region(self, way, n, hop):
        q, s = n // PARTS, lax.rem(n, PARTS)
        if way == 0:
            return lax.rem(self.place.j + 2 * NCOL - q - hop, NCOL), s
        return lax.rem(self.place.j + q + hop, NCOL), lax.rem(s + PARTS // 2, PARTS)

    def copy(self, way, n, hop=0):
        slot, part = self.region(way, n, hop)
        piece = self.held.at[slot, pl.ds(part * PER, PER)]
        return pltpu.make_async_remote_copy(
            src_ref=piece,
            dst_ref=piece,
            send_sem=self.sends.at[way, n],
            recv_sem=self.recvs.at[way, n],
            device_id=self.devices[way],
            device_id_type=MESH,
        )

    def spread(self, slot, first, count):
        def one(b, carry):
            value = self.held[slot, first + b]
            high = value.astype(BF16).astype(F32)
            at = 2 * (slot * STRIPS + first + b) + 1
            both = jnp.concatenate([high, value - high], axis=0).T.astype(BF16)
            self.spread_ref[at] = both[:TILE]
            self.spread_ref[at + 1] = both[TILE:]
            return carry

        lax.fori_loop(0, count, one, 0)

    def run(self, tasks, each):
        def step(n, carry):
            for way in range(2):
                self.copy(way, n, 1).wait_recv()

                @pl.when(n + PARTS < HOPS)
                def forward():
                    self.copy(way, n + PARTS).start()

            for way in range(2):
                slot, part = self.region(way, n, 1)
                self.spread(slot, part * PER, PER)
            each(n)
            return carry

        def end(n, carry):
            for way in range(2):
                self.copy(way, n).wait_send()
            return carry

        done = 0
        for stop, task in tasks:
            lax.fori_loop(done, stop, step, 0)
            task()
            done = stop
        lax.fori_loop(done, HOPS, step, 0)
        lax.fori_loop(0, HOPS, end, 0)


def line(ref):
    value = ref[...].reshape(1, SLOTS)
    return jnp.concatenate([value, jnp.zeros((1, RANKS - SLOTS), I32)], axis=1)


def upright(value):
    return jnp.broadcast_to(value, (LANES, RANKS)).T


def count_of(where, value=1):
    return jnp.sum(jnp.where(where, value, 0), axis=0, keepdims=True)


def order(rows, cols, live):
    lane = lax.broadcasted_iota(I32, (1, RANKS), 1)
    row = jnp.where(lane < live, rows, 255)
    below = lax.broadcasted_iota(I32, (RANKS, LANES), 0)
    row_up = upright(row)
    rank = []
    for b in range(RANKS // LANES):
        here = lax.broadcasted_iota(I32, (RANKS, LANES), 1) + b * LANES
        same = (row_up == row[:, b * LANES : (b + 1) * LANES]) & (below < here)
        rank.append(count_of(same))
    rank = jnp.concatenate(rank, axis=1)
    name = lax.broadcasted_iota(I32, (RANKS, LANES), 1)
    held = count_of(row_up == name)
    pairs = jnp.right_shift(held + 1, 1)
    pairs_up = jnp.broadcast_to(pairs, (LANES, LANES)).T[:ROWS]
    named = lax.broadcasted_iota(I32, (ROWS, RANKS), 0)
    wide_pairs = jnp.concatenate([pairs_up] * (RANKS // LANES), axis=1)
    start = count_of(named < row, wide_pairs)
    place = jnp.where(lane < live, 2 * start + rank, 5000)
    code = lane + 1024 * (cols + 1) + jnp.where(rank == 0, FRESH, 0)
    place_up, code_up = upright(place), upright(code)
    found = []
    for b in range(RANKS // LANES):
        here = lax.broadcasted_iota(I32, (RANKS, LANES), 1) + b * LANES
        found.append(count_of(place_up == here, code_up))
    mine = lax.broadcasted_iota(I32, (ROWS, LANES), 0)
    at = lax.broadcasted_iota(I32, (ROWS, LANES), 1)
    ends = jnp.where(pairs > 0, count_of(mine <= at, pairs_up), 0)
    return jnp.concatenate(found, axis=1), ends


def pack_pair(p, codes, tiles, packed):
    half = jnp.right_shift(lax.broadcasted_iota(I32, (TILE, LANES), 1), 6)

    def one(place, wanted):
        slot = jnp.bitwise_and(codes[0, place], 1023)
        value = tiles[:, pl.ds(jnp.right_shift(slot, 1) * LANES, LANES)]
        odd = jnp.broadcast_to(jnp.bitwise_and(slot, 1), (TILE, LANES))
        return jnp.where(odd == wanted, value, pltpu.roll(value, TILE, 1))

    both = jnp.where(half == 0, one(2 * p, 0), one(2 * p + 1, 1))
    packed[p] = jnp.concatenate(halves(both), axis=1)


def multiply(codes, ends, packed, spread_ref, sums, part, after):
    def batch(s, run):
        found = []
        for u in range(BATCH):
            p = s * BATCH + u
            pair = (codes[0, 2 * p], codes[0, 2 * p + 1])
            tables = []
            for code in pair:
                tables.append(spread_ref[jnp.bitwise_and(jnp.right_shift(code, 10), 255)])
            out = jnp.dot(
                packed[p], jnp.concatenate(tables * 2, axis=0), preferred_element_type=F32
            )
            fresh = jnp.broadcast_to(pair[0], (TILE, LANES)) >= FRESH
            found.append((p, fresh, out))
        for p, fresh, out in found:
            run = jnp.where(fresh, 0.0, run) + out
            sums[p + 1] = run
        return run

    sums[0] = jnp.zeros((TILE, LANES), F32)
    lax.fori_loop(0, PAIRS // BATCH, batch, jnp.zeros((TILE, LANES), F32))

    def place(b, carry):
        both = jnp.concatenate([sums[ends[0, 2 * b]], sums[ends[0, 2 * b + 1]]], axis=0).T
        part[:, pl.ds(pl.multiple_of(b * LANES, LANES), LANES)] = both[:MODES] + both[MODES:]
        return carry

    for third in (0, 2, 1):
        lax.fori_loop(third * STRIPS, (third + 1) * STRIPS, place, 0, unroll=STRIPS)
        after(third)


def correct(place, x, ax, diag, theta_t, w, ring):
    for part, way, n in ((0, 0, 0), (2, 1, 0), (1, 0, 1), (3, 1, 1)):
        for s in range(part * PER, (part + 1) * PER):
            at = slice(s * LANES, (s + 1) * LANES)
            value = (ax[:, at] - product(theta_t, x[:, at], NN)) / diag[:, at]
            w[:, at] = value
            ring.held[place.j, s] = value
        ring.copy(way, n).start()
    for n in (2, 3):
        for way in range(2):
            ring.copy(way, n).start()


def theta_local(x, ax):
    return product(ax[...], x[...], NT) * (1.0 / DOFS)


def fold(value):
    return jnp.concatenate([value[:96], value[96:]], axis=1)


def unfold(value):
    return jnp.concatenate([value[:, :64], value[:, 64:]], axis=0)


def gram_rest(x, w, p, ax, ap, flat, base):
    basis = jnp.concatenate([x[...], w[...], p[...]], axis=0)
    other = jnp.concatenate([ax[...], ap[...], basis], axis=0)
    block = product(basis, other, NT) * (1.0 / DOFS)
    flat[base : base + 192, :] = block[:, :128]
    flat[base + 192 : base + 384, :] = block[:, 128:256]
    flat[base + 384 : base + 480, :] = fold(block[:, 256:])


def gram_image(x, w, p, aw, flat):
    basis = jnp.concatenate([x[...], w[...], p[...]], axis=0)
    flat[0:96, :] = fold(product(basis, aw[...], NT) * (1.0 / DOFS))


def halo_scratch(tag):
    return {
        f"{tag}_above": pltpu.VMEM((MODES, LOCAL), F32),
        f"{tag}_below": pltpu.VMEM((MODES, LOCAL), F32),
        f"{tag}_s": DMA((2,)),
        f"{tag}_r": DMA((2,)),
    }


def halo(place, part, refs, tag, third):
    at = third // 2
    copy = pltpu.make_async_remote_copy(
        src_ref=part.at[:, pl.ds(third * LOCAL, LOCAL)],
        dst_ref=refs[f"{tag}_below" if at else f"{tag}_above"],
        send_sem=refs[f"{tag}_s"].at[at],
        recv_sem=refs[f"{tag}_r"].at[at],
        device_id=place.next_row if at else place.last_row,
        device_id_type=MESH,
    )
    copy.start()
    return copy


def near_scratch():
    shapes = {f"near_{n}": pltpu.VMEM((2, MODES, LOCAL), F32) for n in "xpw"}
    return shapes | {"near_s": DMA((6,)), "near_r": DMA((6,))}


def lend(place, refs, name, field):
    copies = []
    for side, device in enumerate((place.next_row, place.last_row)):
        at = 2 * "xpw".index(name) + side
        copy = pltpu.make_async_remote_copy(
            src_ref=field,
            dst_ref=refs[f"near_{name}"].at[side],
            send_sem=refs["near_s"].at[at],
            recv_sem=refs["near_r"].at[at],
            device_id=device,
            device_id_type=MESH,
        )
        copy.start()
        copies.append(copy)
    return copies


def image(part, w, diag, refs, tag, aw):
    aw[...] = (
        part[:, LOCAL : 2 * LOCAL]
        + refs[f"{tag}_below"][...]
        + refs[f"{tag}_above"][...]
        + diag[...] * w[...]
    )


def rotate(turn, x, w, p, next_x, next_p):
    moved = product(turn[:, 64:], jnp.concatenate([w[...], p[...]], axis=0), NN)
    next_p[...] = moved
    next_x[...] = product(turn[:, :64], x[...], NN) + moved


def put_stiff(rest, image_block, grams, k):
    block = rest[0:192]
    grams[k, 0] = jnp.concatenate([block[:, :64], unfold(image_block), block[:, 64:]], axis=1)


def put_mass(rest, grams, k):
    grams[k, 1] = jnp.concatenate([rest[192:384], unfold(rest[384:480])], axis=1)


FIELDS = ("x", "ax", "diag", "p", "ap")
FIELD = pltpu.VMEM((MODES, LOCAL), F32)
NAMED = Scratch(
    {name: FIELD for name in FIELDS}
    | {f"{n}{k}": FIELD for k in (1, 2) for n in ("x", "p", "ax", "ap")}
    | {name: FIELD for name in ("w", "w1", "aw", "aw1")}
    | {
        "turn": pltpu.VMEM((2, MODES, 3 * MODES), F32),
        "tiles": pltpu.VMEM((TILE, SLOTS * TILE), F32),
        "loads": DMA((7,)),
        "stores": DMA((7,)),
        "codes_v": pltpu.VMEM((1, RANKS), I32),
        "ends_v": pltpu.VMEM((1, LANES), I32),
        "codes": pltpu.SMEM((1, RANKS), I32),
        "ends": pltpu.SMEM((1, LANES), I32),
        "lists": DMA((2,)),
        "packed": pltpu.VMEM((PAIRS, TILE, 2 * LANES), BF16),
        "sums": pltpu.VMEM((PAIRS + 1, TILE, LANES), F32),
        "spread": pltpu.VMEM((BLOCKS + 1, TILE, LANES), BF16),
        "part": pltpu.VMEM((MODES, 3 * LOCAL), F32),
        "flat0": pltpu.VMEM((480, LANES), F32),
        "flat1": pltpu.VMEM((576, LANES), F32),
        "flat2": pltpu.VMEM((96, LANES), F32),
        "grams": pltpu.VMEM((2, 2, 192, 192), F32),
    }
    | {"before_t": pltpu.VMEM((MODES, MODES), F32), "before_g": pltpu.VMEM((192, MODES), F32)}
    | near_scratch()
    | theta_scratch("theta0")
    | theta_scratch("theta1")
    | ring_scratch("ring0")
    | ring_scratch("ring1")
    | halo_scratch("halo0")
    | halo_scratch("halo1")
    | mix_scratch("mix0", 480)
    | mix_scratch("mix1", 576)
    | short_scratch("mix2", 96)
)
BESIDE_Y, BESIDE_Z = 72, 200


def steps(
    rows, cols, count, x_in, ax_in, diag_in, p_in, ap_in, turn_in, tiles_in,
    x_out, p_out, ax_out, ap_out, grams_out, *refs,
):
    place = Place()
    ready = greet(place, rows=True)
    r = NAMED.found(refs)
    loads = {}
    for n, (name, source) in enumerate(
        zip(FIELDS + ("turn", "tiles"), (x_in, ax_in, diag_in, p_in, ap_in, turn_in, tiles_in))
    ):
        loads[name] = pltpu.make_async_copy(source, r[name], r["loads"].at[n])
        loads[name].start()
    stores = []

    def store(source, target):
        copy = pltpu.make_async_copy(source, target, r["stores"].at[len(stores)])
        copy.start()
        stores.append(copy)

    codes, ends, packed, tiles = r["codes"], r["ends"], r["packed"], r["tiles"]
    x, ax, diag, p, ap = (r[name] for name in FIELDS)
    w, w1, aw, aw1, part, spread_ref = (
        r[n] for n in ("w", "w1", "aw", "aw1", "part", "spread")
    )

    def nothing(*unused):
        pass

    def sort():
        code, end = order(line(rows), line(cols), count[0])
        r["codes_v"][...] = code
        r["ends_v"][...] = end
        moves = [
            pltpu.make_async_copy(r["codes_v"], codes, r["lists"].at[0]),
            pltpu.make_async_copy(r["ends_v"], ends, r["lists"].at[1]),
        ]
        for move in moves:
            move.start()
        for move in moves:
            move.wait()
        spread_ref[0] = jnp.zeros((TILE, LANES), BF16)

    def pack(a, b):
        def four(s, carry):
            for u in range(4):
                pack_pair(4 * s + u, codes, tiles, packed)
            return carry

        return lambda: lax.fori_loop(a // 4, b // 4, four, 0)

    def pack_first():
        loads["tiles"].wait()
        pack(0, BESIDE_Y)()

    loads["x"].wait()
    loads["ax"].wait()
    local = theta_local(x, ax)
    ready()
    theta_t = sum_theta(
        place, local, r, "theta0", (sort, pack_first, pack(BESIDE_Y, BESIDE_Z))
    )
    loads["diag"].wait()
    ring = Ring(place, r, "ring0", spread_ref)
    correct(place, x, ax, diag, theta_t, w, ring)
    loads["p"].wait()
    loads["ap"].wait()
    loads["turn"].wait()
    flat0, flat1, flat2, before_t, before_g = (
        r[n] for n in ("flat0", "flat1", "flat2", "before_t", "before_g")
    )
    x1, p1, ax1, ap1 = (r[n] for n in ("x1", "p1", "ax1", "ap1"))
    x2, p2, ax2, ap2 = (r[n] for n in ("x2", "p2", "ax2", "ap2"))
    near_x, near_p, near_w = (r[f"near_{n}"] for n in "xpw")
    mix0 = mix(place, 480, flat0, r, "mix0")
    mix1 = mix(place, 576, flat1, r, "mix1")
    mix2 = mix_short(place, 96, flat2, r, "mix2")
    lent, sent = [], []

    def thirds(n):
        return part[:, n * LOCAL : (n + 1) * LOCAL]

    def own0():
        ring.spread(place.j, 0, STRIPS)
        gram_rest(x, w, p, ax, ap, flat0, 0)
        next(mix0)

    def turn0():
        rotate(r["turn"][0], x, w, p, x1, p1)
        lent.extend(lend(place, r, "x", x1))
        lent.extend(lend(place, r, "p", p1))

    def theta0():
        known = jnp.concatenate([ax[...], diag[...] * w[...], ap[...]], axis=0)
        before_t[...] = product(product(r["turn"][0], known, NN), x1[...], NT)

    def each0(n):
        for u in range(8):
            pack_pair(BESIDE_Z + n * 8 + u, codes, tiles, packed)

    def send(tag):
        return lambda third: third == 1 or sent.append(halo(place, part, r, tag, third))

    ring.run(((0, own0), (3, turn0), (6, lambda: next(mix0)), (8, theta0)), each0)
    next(mix0)
    multiply(codes, ends, packed, spread_ref, r["sums"], part, send("halo0"))
    next(mix0)
    finish(lent)
    core = (
        product(thirds(0), near_x[0], NT)
        + product(thirds(2), near_x[1], NT)
        + product(thirds(1), x1[...], NT)
    )
    local = before_t[...] + product(r["turn"][0][:, 64:128], core, NN)

    def images0():
        finish(sent)
        image(part, w, diag, r, "halo0", aw)
        rotate(r["turn"][0], ax, aw, ap, ax1, ap1)

    def grams0():
        gram_image(x, w, p, aw, flat1)

    theta_t = sum_theta(
        place, local * (1.0 / DOFS), r, "theta1", (nothing, images0, grams0)
    )
    ring = Ring(place, r, "ring1", spread_ref)
    correct(place, x1, ax1, diag, theta_t, w1, ring)
    lent, sent = [], []

    def own1():
        lent.extend(lend(place, r, "w", w1))
        ring.spread(place.j, 0, STRIPS)
        gram_rest(x1, w1, p1, ax1, ap1, flat1, 96)
        next(mix1)

    def turn1():
        rotate(r["turn"][1], x1, w1, p1, x2, p2)
        store(x2, x_out)
        store(p2, p_out)

    def image1():
        basis = jnp.concatenate([x1[...], w1[...], p1[...]], axis=0)
        before_g[...] = product(basis, diag[...] * w1[...], NT)

    def both():
        next(mix0)
        next(mix1)

    ring.run(
        ((0, own1), (3, turn1), (5, lambda: next(mix0)), (7, image1), (9, both)), nothing
    )
    next(mix1)
    multiply(codes, ends, packed, spread_ref, r["sums"], part, send("halo1"))
    next(mix1)
    finish(lent)
    total_image = before_g[...]
    for third, fields in (
        (0, (near_x[0], near_w[0], near_p[0])),
        (1, (x1[...], w1[...], p1[...])),
        (2, (near_x[1], near_w[1], near_p[1])),
    ):
        total_image += product(jnp.concatenate(fields, axis=0), thirds(third), NT)
    flat2[...] = fold(total_image * (1.0 / DOFS))
    next(mix2)
    next(mix2)
    finish(sent)
    image(part, w1, diag, r, "halo1", aw1)
    next(mix2)
    next(mix1)
    rotate(r["turn"][1], ax1, aw1, ap1, ax2, ap2)
    store(ax2, ax_out)
    store(ap2, ap_out)
    next(mix1)
    put_stiff(flat0[...], flat1[0:96], r["grams"], 0)
    put_mass(flat0[...], r["grams"], 0)
    store(r["grams"].at[0], grams_out.at[0])
    put_mass(flat1[96:576], r["grams"], 1)
    store(r["grams"].at[1, 1], grams_out.at[1, 1])
    next(mix2)
    next(mix2)
    put_stiff(flat1[96:576], flat2[...], r["grams"], 1)
    store(r["grams"].at[1, 0], grams_out.at[1, 0])
    for copy in stores:
        copy.wait()


def body(x, p, ax, ap, diag, tiles, rows, cols, count, turns):
    field = jax.ShapeDtypeStruct((MODES, LOCAL), F32)
    far = pl.BlockSpec(memory_space=pl.ANY)
    found = pl.pallas_call(
        steps,
        out_shape=[field] * 4 + [jax.ShapeDtypeStruct((2, 2, 192, 192), F32)],
        in_specs=[
            pl.BlockSpec(memory_space=pltpu.VMEM),
            pl.BlockSpec(memory_space=pltpu.VMEM),
            pl.BlockSpec(memory_space=pltpu.SMEM),
        ]
        + [far] * 7,
        out_specs=[far] * 5,
        scratch_shapes=NAMED.shapes,
        compiler_params=pltpu.CompilerParams(
            collective_id=1, has_side_effects=True, vmem_limit_bytes=60 << 20
        ),
        name="steps",
    )(rows, cols, count, x, ax, diag, p, ap, turns.swapaxes(1, 2), tiles)
    return pl.pallas_call(
        hand_over,
        out_shape=[jax.ShapeDtypeStruct(f.shape, f.dtype) for f in found],
        in_specs=[far] * 5,
        out_specs=[far] * 5,
        scratch_shapes=[pltpu.VMEM(f.shape, f.dtype) for f in found] + [DMA((5,))] * 2,
        compiler_params=pltpu.CompilerParams(vmem_limit_bytes=60 << 20),
        name="hand_over",
    )(*found)


def hand_over(*refs):
    given, wanted, held, (inward, outward) = refs[:5], refs[5:10], refs[10:15], refs[15:]
    first = [pltpu.make_async_copy(given[n], held[n], inward.at[n]) for n in range(5)]
    last = [pltpu.make_async_copy(held[n], wanted[n], outward.at[n]) for n in range(5)]
    for copy in first:
        copy.start()
    for n in range(5):
        first[n].wait()
        last[n].start()
    for copy in last:
        copy.wait()


def solution(mesh):
    split = P(None, ("row", "col"))
    listed = P(("row", "col"))
    return jax.shard_map(
        lambda *args: tuple(body(*args)),
        mesh=mesh,
        in_specs=(split,) * 6 + (listed,) * 3 + (P(),),
        out_specs=(split,) * 4 + (P(),),
        check_vma=False,
    )
```

```python
import functools

import jax
import jax.numpy as jnp
from jax import lax
from jax.experimental import pallas as pl
from jax.experimental.pallas import tpu as pltpu
from jax.sharding import PartitionSpec as P

F32 = jnp.float32
I32 = jnp.int32
BF16 = jnp.bfloat16
MESH = pl.DeviceIdType.MESH
DMA = pltpu.SemaphoreType.DMA

MODES, TILE, BPD, SLOTS = 64, 64, 16, 576
NROW, NCOL = 32, 8
LOCAL = TILE * BPD
DOFS = LOCAL * NROW * NCOL
PLANE, DEEP = 8, 4
SIZES = {"xc": PLANE, "y": DEEP, "z": NCOL}
LANES = 128
STRIPS = LOCAL // LANES
BLOCKS = NCOL * BPD
ROWS = 3 * BPD
PARTS = 4
HOPS = 3 * PARTS + PARTS // 2
PER = STRIPS // PARTS
RANKS = 640
PAIRS = SLOTS // 2 + ROWS // 2
BATCH = 156
FRESH = 1 << 18


def halves(value):
    high = value.astype(BF16)
    return high, (value - high.astype(F32)).astype(BF16)


def product(a, b, dims):
    return split_product(halves(a), halves(b), dims)


def split_product(a, b, dims):
    dot = functools.partial(
        lax.dot_general, dimension_numbers=(dims, ((), ())), preferred_element_type=F32
    )
    (a_high, a_low), (b_high, b_low) = a, b
    return dot(a_high, b_high) + (dot(a_high, b_low) + dot(a_low, b_high))


NN = ((1,), (0,))
NT = ((1,), (1,))
TN = ((0,), (0,))


class Place:
    def __init__(self):
        i, j = lax.axis_index("row"), lax.axis_index("col")
        self.i, self.j = i, j
        plane, inner = i // PLANE, lax.rem(i, PLANE)
        self.groups = {
            "xc": (PLANE, inner, lambda m: (plane * PLANE + m, j)),
            "y": (DEEP, plane, lambda m: (m * PLANE + inner, j)),
            "z": (NCOL, j, lambda m: (i, m)),
        }
        self.next_row = (lax.rem(i + 1, NROW), j)
        self.last_row = (lax.rem(i + NROW - 1, NROW), j)
        self.right = (i, lax.rem(j + 1, NCOL))
        self.left = (i, lax.rem(j + NCOL - 1, NCOL))


def greet(place, rows):
    barrier = pltpu.get_barrier_semaphore()
    devices = [place.next_row, place.last_row] if rows else []
    for size, me, device in place.groups.values():
        devices += [device(lax.rem(me + o, size)) for o in range(1, size)]
    for device in devices:
        pl.semaphore_signal(barrier, inc=1, device_id=device, device_id_type=MESH)
    return lambda: pl.semaphore_wait(barrier, len(devices))


def swap(place, name, source, landing, sends, recvs):
    size, me, device = place.groups[name]
    copies = []
    for o in range(1, size):
        peer = lax.rem(me + o, size)
        copy = pltpu.make_async_remote_copy(
            src_ref=source(peer),
            dst_ref=landing.at[me],
            send_sem=sends.at[o],
            recv_sem=recvs.at[o],
            device_id=device(peer),
            device_id_type=MESH,
        )
        copy.start()
        copies.append(copy)
    return copies


def finish(copies):
    for copy in copies:
        copy.wait()


def total(landing):
    value = landing[0]
    for m in range(1, landing.shape[0]):
        value = value + landing[m]
    return value


class Scratch:
    def __init__(self, shapes):
        self.names, self.shapes = list(shapes), list(shapes.values())

    def found(self, refs):
        return dict(zip(self.names, refs))


def sum_theta(place, local, refs, tag, work):
    value = jnp.concatenate([local[:32], local[32:]], axis=1)
    for at, name in enumerate(SIZES):
        landing = refs[f"{tag}_{name}"]
        me = place.groups[name][1]
        landing[me] = value
        copies = swap(
            place,
            name,
            lambda peer: landing.at[me],
            landing,
            refs[f"{tag}_{name}_s"],
            refs[f"{tag}_{name}_r"],
        )
        work[at]()
        finish(copies)
        value = total(landing)
    return jnp.concatenate([value[:, :64], value[:, 64:]], axis=0)


def theta_scratch(tag):
    shapes = {}
    for name, size in SIZES.items():
        shapes[f"{tag}_{name}"] = pltpu.VMEM((size, 32, LANES), F32)
        shapes[f"{tag}_{name}_s"] = DMA((size,))
        shapes[f"{tag}_{name}_r"] = DMA((size,))
    return shapes


STAGES = ("xc", "y", "z", "y", "xc")


def mix_scratch(tag, rows):
    r = rows // NROW
    big, mid = (PLANE, DEEP, r, LANES), (DEEP, r, LANES)
    shapes = {
        f"{tag}_{n}": pltpu.VMEM(s, F32)
        for n, s in enumerate((big, big, mid, mid, (NCOL, r, LANES), mid, big))
    }
    for n, name in enumerate(STAGES):
        shapes[f"{tag}_s{n}"] = DMA((SIZES[name],))
        shapes[f"{tag}_r{n}"] = DMA((SIZES[name],))
    return shapes


def mix(place, rows, flat, refs, tag):
    r = rows // NROW
    data, land_a, half, land_b, land_z, back, result = (refs[f"{tag}_{n}"] for n in range(7))
    sems = [(refs[f"{tag}_s{n}"], refs[f"{tag}_r{n}"]) for n in range(5)]
    mine = {name: place.groups[name][1] for name in SIZES}
    for a in range(PLANE):
        for b in range(DEEP):
            at = (a * DEEP + b) * r
            data[a, b] = flat[at : at + r, :]
    land_a[mine["xc"]] = data[mine["xc"]]
    copies = swap(place, "xc", lambda peer: data.at[peer], land_a, *sems[0])
    yield
    finish(copies)
    half[...] = total(land_a)
    land_b[mine["y"]] = half[mine["y"]]
    copies = swap(place, "y", lambda peer: half.at[peer], land_b, *sems[1])
    yield
    finish(copies)
    land_z[mine["z"]] = total(land_b)
    copies = swap(place, "z", lambda peer: land_z.at[mine["z"]], land_z, *sems[2])
    yield
    finish(copies)
    back[mine["y"]] = total(land_z)
    copies = swap(place, "y", lambda peer: back.at[mine["y"]], back, *sems[3])
    yield
    finish(copies)
    result[mine["xc"]] = back[...]
    copies = swap(place, "xc", lambda peer: result.at[mine["xc"]], result, *sems[4])
    yield
    finish(copies)
    for a in range(PLANE):
        for b in range(DEEP):
            at = (a * DEEP + b) * r
            flat[at : at + r, :] = result[a, b]
    yield


def short_scratch(tag, rows):
    r = rows // PLANE
    shapes = {
        f"{tag}_{n}": pltpu.VMEM((size, r, LANES), F32)
        for n, size in enumerate((PLANE, PLANE, DEEP, NCOL, PLANE))
    }
    for n, name in enumerate(("xc", "y", "z", "xc")):
        shapes[f"{tag}_s{n}"] = DMA((SIZES[name],))
        shapes[f"{tag}_r{n}"] = DMA((SIZES[name],))
    return shapes


def mix_short(place, rows, flat, refs, tag):
    r = rows // PLANE
    data, land_a, land_b, land_z, result = (refs[f"{tag}_{n}"] for n in range(5))
    sems = [(refs[f"{tag}_s{n}"], refs[f"{tag}_r{n}"]) for n in range(4)]
    mine = {name: place.groups[name][1] for name in SIZES}
    for a in range(PLANE):
        data[a] = flat[a * r : (a + 1) * r, :]
    land_a[mine["xc"]] = data[mine["xc"]]
    copies = swap(place, "xc", lambda peer: data.at[peer], land_a, *sems[0])
    yield
    finish(copies)
    land_b[mine["y"]] = total(land_a)
    copies = swap(place, "y", lambda peer: land_b.at[mine["y"]], land_b, *sems[1])
    yield
    finish(copies)
    land_z[mine["z"]] = total(land_b)
    copies = swap(place, "z", lambda peer: land_z.at[mine["z"]], land_z, *sems[2])
    yield
    finish(copies)
    result[mine["xc"]] = total(land_z)
    copies = swap(place, "xc", lambda peer: result.at[mine["xc"]], result, *sems[3])
    yield
    finish(copies)
    for a in range(PLANE):
        flat[a * r : (a + 1) * r, :] = result[a]
    yield


def ring_scratch(tag):
    return {
        f"{tag}_held": pltpu.VMEM((NCOL, STRIPS, MODES, LANES), F32),
        f"{tag}_s": DMA((2, HOPS)),
        f"{tag}_r": DMA((2, HOPS)),
    }


class Ring:
    def __init__(self, place, refs, tag, spread_ref):
        self.place, self.spread_ref = place, spread_ref
        self.held, self.sends, self.recvs = (refs[f"{tag}_{n}"] for n in ("held", "s", "r"))
        self.devices = (place.right, place.left)

    def region(self, way, n, hop):
        q, s = n // PARTS, lax.rem(n, PARTS)
        if way == 0:
            return lax.rem(self.place.j + 2 * NCOL - q - hop, NCOL), s
        return lax.rem(self.place.j + q + hop, NCOL), lax.rem(s + PARTS // 2, PARTS)

    def copy(self, way, n, hop=0):
        slot, part = self.region(way, n, hop)
        piece = self.held.at[slot, pl.ds(part * PER, PER)]
        return pltpu.make_async_remote_copy(
            src_ref=piece,
            dst_ref=piece,
            send_sem=self.sends.at[way, n],
            recv_sem=self.recvs.at[way, n],
            device_id=self.devices[way],
            device_id_type=MESH,
        )

    def spread(self, slot, first, count):
        def one(b, carry):
            value = self.held[slot, first + b]
            high = value.astype(BF16).astype(F32)
            at = 2 * (slot * STRIPS + first + b) + 1
            both = jnp.concatenate([high, value - high], axis=0).T.astype(BF16)
            self.spread_ref[at] = both[:TILE]
            self.spread_ref[at + 1] = both[TILE:]
            return carry

        lax.fori_loop(0, count, one, 0)

    def run(self, tasks, each):
        def step(n, carry):
            for way in range(2):
                self.copy(way, n, 1).wait_recv()

                @pl.when(n + PARTS < HOPS)
                def forward():
                    self.copy(way, n + PARTS).start()

            for way in range(2):
                slot, part = self.region(way, n, 1)
                self.spread(slot, part * PER, PER)
            each(n)
            return carry

        def end(n, carry):
            for way in range(2):
                self.copy(way, n).wait_send()
            return carry

        done = 0
        for stop, task in tasks:
            lax.fori_loop(done, stop, step, 0)
            task()
            done = stop
        lax.fori_loop(done, HOPS, step, 0)
        lax.fori_loop(0, HOPS, end, 0)


def line(ref):
    value = ref[...].reshape(1, SLOTS)
    return jnp.concatenate([value, jnp.zeros((1, RANKS - SLOTS), I32)], axis=1)


def upright(value):
    return jnp.broadcast_to(value, (LANES, RANKS)).T


def count_of(where, value=1):
    return jnp.sum(jnp.where(where, value, 0), axis=0, keepdims=True)


def order(rows, cols, live):
    lane = lax.broadcasted_iota(I32, (1, RANKS), 1)
    row = jnp.where(lane < live, rows, 255)
    below = lax.broadcasted_iota(I32, (RANKS, LANES), 0)
    row_up = upright(row)
    rank = []
    for b in range(RANKS // LANES):
        here = lax.broadcasted_iota(I32, (RANKS, LANES), 1) + b * LANES
        same = (row_up == row[:, b * LANES : (b + 1) * LANES]) & (below < here)
        rank.append(count_of(same))
    rank = jnp.concatenate(rank, axis=1)
    name = lax.broadcasted_iota(I32, (RANKS, LANES), 1)
    held = count_of(row_up == name)
    pairs = jnp.right_shift(held + 1, 1)
    pairs_up = jnp.broadcast_to(pairs, (LANES, LANES)).T[:ROWS]
    named = lax.broadcasted_iota(I32, (ROWS, RANKS), 0)
    wide_pairs = jnp.concatenate([pairs_up] * (RANKS // LANES), axis=1)
    start = count_of(named < row, wide_pairs)
    place = jnp.where(lane < live, 2 * start + rank, 5000)
    code = lane + 1024 * (cols + 1) + jnp.where(rank == 0, FRESH, 0)
    place_up, code_up = upright(place), upright(code)
    found = []
    for b in range(RANKS // LANES):
        here = lax.broadcasted_iota(I32, (RANKS, LANES), 1) + b * LANES
        found.append(count_of(place_up == here, code_up))
    mine = lax.broadcasted_iota(I32, (ROWS, LANES), 0)
    at = lax.broadcasted_iota(I32, (ROWS, LANES), 1)
    ends = jnp.where(pairs > 0, count_of(mine <= at, pairs_up), 0)
    return jnp.concatenate(found, axis=1), ends


def pack_pair(p, codes, tiles, packed):
    half = jnp.right_shift(lax.broadcasted_iota(I32, (TILE, LANES), 1), 6)

    def one(place, wanted):
        slot = jnp.bitwise_and(codes[0, place], 1023)
        value = tiles[:, pl.ds(jnp.right_shift(slot, 1) * LANES, LANES)]
        odd = jnp.broadcast_to(jnp.bitwise_and(slot, 1), (TILE, LANES))
        return jnp.where(odd == wanted, value, pltpu.roll(value, TILE, 1))

    both = jnp.where(half == 0, one(2 * p, 0), one(2 * p + 1, 1))
    packed[p] = jnp.concatenate(halves(both), axis=1)


def multiply(codes, ends, packed, spread_ref, sums, part, after):
    def batch(s, run):
        found = []
        for u in range(BATCH):
            p = s * BATCH + u
            pair = (codes[0, 2 * p], codes[0, 2 * p + 1])
            tables = []
            for code in pair:
                tables.append(spread_ref[jnp.bitwise_and(jnp.right_shift(code, 10), 255)])
            out = jnp.dot(
                packed[p], jnp.concatenate(tables * 2, axis=0), preferred_element_type=F32
            )
            fresh = jnp.broadcast_to(pair[0], (TILE, LANES)) >= FRESH
            found.append((p, fresh, out))
        for p, fresh, out in found:
            run = jnp.where(fresh, 0.0, run) + out
            sums[p + 1] = run
        return run

    sums[0] = jnp.zeros((TILE, LANES), F32)
    lax.fori_loop(0, PAIRS // BATCH, batch, jnp.zeros((TILE, LANES), F32))

    def place(b, carry):
        both = jnp.concatenate([sums[ends[0, 2 * b]], sums[ends[0, 2 * b + 1]]], axis=0).T
        part[:, pl.ds(pl.multiple_of(b * LANES, LANES), LANES)] = both[:MODES] + both[MODES:]
        return carry

    for third in (0, 2, 1):
        lax.fori_loop(third * STRIPS, (third + 1) * STRIPS, place, 0, unroll=STRIPS)
        after(third)


def correct(place, x, ax, diag, theta_t, w, ring):
    for part, way, n in ((0, 0, 0), (2, 1, 0), (1, 0, 1), (3, 1, 1)):
        for s in range(part * PER, (part + 1) * PER):
            at = slice(s * LANES, (s + 1) * LANES)
            value = (ax[:, at] - product(theta_t, x[:, at], NN)) / diag[:, at]
            w[:, at] = value
            ring.held[place.j, s] = value
        ring.copy(way, n).start()
    for n in (2, 3):
        for way in range(2):
            ring.copy(way, n).start()


def theta_local(x, ax):
    return product(ax[...], x[...], NT) * (1.0 / DOFS)


def fold(value):
    return jnp.concatenate([value[:96], value[96:]], axis=1)


def unfold(value):
    return jnp.concatenate([value[:, :64], value[:, 64:]], axis=0)


def gram_rest(x, w, p, ax, ap, flat, base):
    basis = jnp.concatenate([x[...], w[...], p[...]], axis=0)
    other = jnp.concatenate([ax[...], ap[...], basis], axis=0)
    block = product(basis, other, NT) * (1.0 / DOFS)
    flat[base : base + 192, :] = block[:, :128]
    flat[base + 192 : base + 384, :] = block[:, 128:256]
    flat[base + 384 : base + 480, :] = fold(block[:, 256:])


def gram_image(x, w, p, aw, flat):
    basis = jnp.concatenate([x[...], w[...], p[...]], axis=0)
    flat[0:96, :] = fold(product(basis, aw[...], NT) * (1.0 / DOFS))


def halo_scratch(tag):
    return {
        f"{tag}_above": pltpu.VMEM((MODES, LOCAL), F32),
        f"{tag}_below": pltpu.VMEM((MODES, LOCAL), F32),
        f"{tag}_s": DMA((2,)),
        f"{tag}_r": DMA((2,)),
    }


def halo(place, part, refs, tag, third):
    at = third // 2
    copy = pltpu.make_async_remote_copy(
        src_ref=part.at[:, pl.ds(third * LOCAL, LOCAL)],
        dst_ref=refs[f"{tag}_below" if at else f"{tag}_above"],
        send_sem=refs[f"{tag}_s"].at[at],
        recv_sem=refs[f"{tag}_r"].at[at],
        device_id=place.next_row if at else place.last_row,
        device_id_type=MESH,
    )
    copy.start()
    return copy


def near_scratch():
    shapes = {f"near_{n}": pltpu.VMEM((2, MODES, LOCAL), F32) for n in "xpw"}
    return shapes | {"near_s": DMA((6,)), "near_r": DMA((6,))}


def lend(place, refs, name, field):
    copies = []
    for side, device in enumerate((place.next_row, place.last_row)):
        at = 2 * "xpw".index(name) + side
        copy = pltpu.make_async_remote_copy(
            src_ref=field,
            dst_ref=refs[f"near_{name}"].at[side],
            send_sem=refs["near_s"].at[at],
            recv_sem=refs["near_r"].at[at],
            device_id=device,
            device_id_type=MESH,
        )
        copy.start()
        copies.append(copy)
    return copies


def image(part, w, diag, refs, tag, aw):
    aw[...] = (
        part[:, LOCAL : 2 * LOCAL]
        + refs[f"{tag}_below"][...]
        + refs[f"{tag}_above"][...]
        + diag[...] * w[...]
    )


def rotate(turn, x, w, p, next_x, next_p):
    moved = product(turn[:, 64:], jnp.concatenate([w[...], p[...]], axis=0), NN)
    next_p[...] = moved
    next_x[...] = product(turn[:, :64], x[...], NN) + moved


def put_stiff(rest, image_block, grams, k):
    block = rest[0:192]
    grams[k, 0] = jnp.concatenate([block[:, :64], unfold(image_block), block[:, 64:]], axis=1)


def put_mass(rest, grams, k):
    grams[k, 1] = jnp.concatenate([rest[192:384], unfold(rest[384:480])], axis=1)


FIELDS = ("x", "ax", "diag", "p", "ap")
FIELD = pltpu.VMEM((MODES, LOCAL), F32)
NAMED = Scratch(
    {name: FIELD for name in FIELDS}
    | {f"{n}{k}": FIELD for k in (1, 2) for n in ("x", "p", "ax", "ap")}
    | {name: FIELD for name in ("w", "w1", "aw", "aw1")}
    | {
        "turn": pltpu.VMEM((2, MODES, 3 * MODES), F32),
        "tiles": pltpu.VMEM((TILE, SLOTS * TILE), F32),
        "loads": DMA((7,)),
        "stores": DMA((7,)),
        "codes_v": pltpu.VMEM((1, RANKS), I32),
        "ends_v": pltpu.VMEM((1, LANES), I32),
        "codes": pltpu.SMEM((1, RANKS), I32),
        "ends": pltpu.SMEM((1, LANES), I32),
        "lists": DMA((2,)),
        "packed": pltpu.VMEM((PAIRS, TILE, 2 * LANES), BF16),
        "sums": pltpu.VMEM((PAIRS + 1, TILE, LANES), F32),
        "spread": pltpu.VMEM((BLOCKS + 1, TILE, LANES), BF16),
        "part": pltpu.VMEM((MODES, 3 * LOCAL), F32),
        "flat0": pltpu.VMEM((480, LANES), F32),
        "flat1": pltpu.VMEM((576, LANES), F32),
        "flat2": pltpu.VMEM((96, LANES), F32),
        "grams": pltpu.VMEM((2, 2, 192, 192), F32),
    }
    | {"before_t": pltpu.VMEM((MODES, MODES), F32), "before_g": pltpu.VMEM((192, MODES), F32)}
    | {f"s_{n}": pltpu.VMEM((3, 3 * MODES, LOCAL), BF16) for n in ("high", "low")}
    | near_scratch()
    | theta_scratch("theta0")
    | theta_scratch("theta1")
    | ring_scratch("ring0")
    | ring_scratch("ring1")
    | halo_scratch("halo0")
    | halo_scratch("halo1")
    | mix_scratch("mix0", 480)
    | mix_scratch("mix1", 576)
    | short_scratch("mix2", 96)
)
BESIDE_Y, BESIDE_Z = 72, 200


def steps(
    rows, cols, count, x_in, ax_in, diag_in, p_in, ap_in, turn_in, tiles_in,
    x_out, p_out, ax_out, ap_out, grams_out, *refs,
):
    place = Place()
    ready = greet(place, rows=True)
    r = NAMED.found(refs)
    loads = {}
    for n, (name, source) in enumerate(
        zip(FIELDS + ("turn", "tiles"), (x_in, ax_in, diag_in, p_in, ap_in, turn_in, tiles_in))
    ):
        loads[name] = pltpu.make_async_copy(source, r[name], r["loads"].at[n])
        loads[name].start()
    stores = []

    def store(source, target):
        copy = pltpu.make_async_copy(source, target, r["stores"].at[len(stores)])
        copy.start()
        stores.append(copy)

    codes, ends, packed, tiles = r["codes"], r["ends"], r["packed"], r["tiles"]
    x, ax, diag, p, ap = (r[name] for name in FIELDS)
    w, w1, aw, aw1, part, spread_ref = (
        r[n] for n in ("w", "w1", "aw", "aw1", "part", "spread")
    )

    def nothing(*unused):
        pass

    def sort():
        code, end = order(line(rows), line(cols), count[0])
        r["codes_v"][...] = code
        r["ends_v"][...] = end
        moves = [
            pltpu.make_async_copy(r["codes_v"], codes, r["lists"].at[0]),
            pltpu.make_async_copy(r["ends_v"], ends, r["lists"].at[1]),
        ]
        for move in moves:
            move.start()
        for move in moves:
            move.wait()
        spread_ref[0] = jnp.zeros((TILE, LANES), BF16)

    def pack(a, b):
        def four(s, carry):
            for u in range(4):
                pack_pair(4 * s + u, codes, tiles, packed)
            return carry

        return lambda: lax.fori_loop(a // 4, b // 4, four, 0)

    def pack_first():
        loads["tiles"].wait()
        pack(0, BESIDE_Y)()

    loads["x"].wait()
    loads["ax"].wait()
    local = theta_local(x, ax)
    ready()
    theta_t = sum_theta(
        place, local, r, "theta0", (sort, pack_first, pack(BESIDE_Y, BESIDE_Z))
    )
    loads["diag"].wait()
    ring = Ring(place, r, "ring0", spread_ref)
    correct(place, x, ax, diag, theta_t, w, ring)
    loads["p"].wait()
    loads["ap"].wait()
    loads["turn"].wait()
    flat0, flat1, flat2, before_t, before_g = (
        r[n] for n in ("flat0", "flat1", "flat2", "before_t", "before_g")
    )
    x1, p1, ax1, ap1 = (r[n] for n in ("x1", "p1", "ax1", "ap1"))
    x2, p2, ax2, ap2 = (r[n] for n in ("x2", "p2", "ax2", "ap2"))
    near_x, near_p, near_w = (r[f"near_{n}"] for n in "xpw")
    s_high, s_low = r["s_high"], r["s_low"]
    mix0 = mix(place, 480, flat0, r, "mix0")
    mix1 = mix(place, 576, flat1, r, "mix1")
    mix2 = mix_short(place, 96, flat2, r, "mix2")
    lent, sent = [], []

    def thirds(n):
        return part[:, n * LOCAL : (n + 1) * LOCAL]

    def own0():
        ring.spread(place.j, 0, STRIPS)
        gram_rest(x, w, p, ax, ap, flat0, 0)
        next(mix0)

    def turn0():
        rotate(r["turn"][0], x, w, p, x1, p1)
        lent.extend(lend(place, r, "x", x1))
        lent.extend(lend(place, r, "p", p1))

    def theta0():
        known = jnp.concatenate([ax[...], diag[...] * w[...], ap[...]], axis=0)
        before_t[...] = product(product(r["turn"][0], known, NN), x1[...], NT)

    def each0(n):
        for u in range(8):
            pack_pair(BESIDE_Z + n * 8 + u, codes, tiles, packed)

    def keep(high, low, third, fields):
        high[third], low[third] = halves(jnp.concatenate(fields, axis=0))

    def kept(high, low, third):
        return (high[third], low[third]), halves(thirds(third))

    def send(tag):
        return lambda third: third == 1 or sent.append(halo(place, part, r, tag, third))

    ring.run(((0, own0), (3, turn0), (6, lambda: next(mix0)), (8, theta0)), each0)
    next(mix0)
    multiply(codes, ends, packed, spread_ref, r["sums"], part, send("halo0"))
    next(mix0)
    finish(lent)
    core = (
        product(thirds(0), near_x[0], NT)
        + product(thirds(2), near_x[1], NT)
        + product(thirds(1), x1[...], NT)
    )
    local = before_t[...] + product(r["turn"][0][:, 64:128], core, NN)

    def images0():
        finish(sent)
        image(part, w, diag, r, "halo0", aw)
        rotate(r["turn"][0], ax, aw, ap, ax1, ap1)
        gram_image(x, w, p, aw, flat1)

    theta_t = sum_theta(
        place, local * (1.0 / DOFS), r, "theta1", (nothing, nothing, images0)
    )
    ring = Ring(place, r, "ring1", spread_ref)
    correct(place, x1, ax1, diag, theta_t, w1, ring)
    lent, sent = [], []

    def own1():
        lent.extend(lend(place, r, "w", w1))
        ring.spread(place.j, 0, STRIPS)
        gram_rest(x1, w1, p1, ax1, ap1, flat1, 96)
        next(mix1)

    def turn1():
        rotate(r["turn"][1], x1, w1, p1, x2, p2)
        store(x2, x_out)
        store(p2, p_out)

    def image1():
        basis = jnp.concatenate([x1[...], w1[...], p1[...]], axis=0)
        before_g[...] = product(basis, diag[...] * w1[...], NT)

    def keep1():
        finish(lent)
        keep(s_high, s_low, 0, [near_x[0], near_w[0], near_p[0]])
        keep(s_high, s_low, 1, [x1[...], w1[...], p1[...]])
        keep(s_high, s_low, 2, [near_x[1], near_w[1], near_p[1]])

    def both():
        next(mix0)
        next(mix1)

    ring.run(
        ((0, own1), (3, turn1), (5, lambda: next(mix0)), (7, image1), (9, both), (11, keep1)),
        nothing,
    )
    next(mix1)
    multiply(codes, ends, packed, spread_ref, r["sums"], part, send("halo1"))
    next(mix1)
    total_image = before_g[...] + sum(
        split_product(*kept(s_high, s_low, n), NT) for n in range(3)
    )
    flat2[...] = fold(total_image * (1.0 / DOFS))
    next(mix2)
    next(mix2)
    next(mix2)
    next(mix1)
    finish(sent)
    image(part, w1, diag, r, "halo1", aw1)
    rotate(r["turn"][1], ax1, aw1, ap1, ax2, ap2)
    store(ax2, ax_out)
    store(ap2, ap_out)
    next(mix1)
    put_stiff(flat0[...], flat1[0:96], r["grams"], 0)
    put_mass(flat0[...], r["grams"], 0)
    store(r["grams"].at[0], grams_out.at[0])
    put_mass(flat1[96:576], r["grams"], 1)
    store(r["grams"].at[1, 1], grams_out.at[1, 1])
    next(mix2)
    next(mix2)
    put_stiff(flat1[96:576], flat2[...], r["grams"], 1)
    store(r["grams"].at[1, 0], grams_out.at[1, 0])
    for copy in stores:
        copy.wait()


def body(x, p, ax, ap, diag, tiles, rows, cols, count, turns):
    field = jax.ShapeDtypeStruct((MODES, LOCAL), F32)
    far = pl.BlockSpec(memory_space=pl.ANY)
    found = pl.pallas_call(
        steps,
        out_shape=[field] * 4 + [jax.ShapeDtypeStruct((2, 2, 192, 192), F32)],
        in_specs=[
            pl.BlockSpec(memory_space=pltpu.VMEM),
            pl.BlockSpec(memory_space=pltpu.VMEM),
            pl.BlockSpec(memory_space=pltpu.SMEM),
        ]
        + [far] * 7,
        out_specs=[far] * 5,
        scratch_shapes=NAMED.shapes,
        compiler_params=pltpu.CompilerParams(
            collective_id=1, has_side_effects=True, vmem_limit_bytes=60 << 20
        ),
        name="steps",
    )(rows, cols, count, x, ax, diag, p, ap, turns.swapaxes(1, 2), tiles)
    return pl.pallas_call(
        hand_over,
        out_shape=[jax.ShapeDtypeStruct(f.shape, f.dtype) for f in found],
        in_specs=[far] * 5,
        out_specs=[far] * 5,
        scratch_shapes=[pltpu.VMEM(f.shape, f.dtype) for f in found] + [DMA((5,))] * 2,
        compiler_params=pltpu.CompilerParams(vmem_limit_bytes=60 << 20),
        name="hand_over",
    )(*found)


def hand_over(*refs):
    given, wanted, held, (inward, outward) = refs[:5], refs[5:10], refs[10:15], refs[15:]
    first = [pltpu.make_async_copy(given[n], held[n], inward.at[n]) for n in range(5)]
    last = [pltpu.make_async_copy(held[n], wanted[n], outward.at[n]) for n in range(5)]
    for copy in first:
        copy.start()
    for n in range(5):
        first[n].wait()
        last[n].start()
    for copy in last:
        copy.wait()


def solution(mesh):
    split = P(None, ("row", "col"))
    listed = P(("row", "col"))
    return jax.shard_map(
        lambda *args: tuple(body(*args)),
        mesh=mesh,
        in_specs=(split,) * 6 + (listed,) * 3 + (P(),),
        out_specs=(split,) * 4 + (P(),),
        check_vma=False,
    )
```
